32 devices in a mesh: gx: 2 (over core), gy: 4 (over y, x), gz: 4 (over z).
Axes of the slice: x: 2, y: 2, z: 4, core: 2. Of those that a mesh axis runs over, the one named last changes fastest.
Arguments:
- velocity: float32 [3, 16, 128, 512], P(None, 'gx', 'gy', 'gz'), may hold values from -6 to 6
- nu_tilde: float32 [16, 128, 512], P('gx', 'gy', 'gz'), may hold values from 0.05 to 2
- fluid_cells: int32 [16, 128, 512], P('gx', 'gy', 'gz'), may hold values 0 or 1
- surface: float32 [2, 4, 3, 512], P('gx', 'gz', None, 'gy'), may hold values from -64 to 64
- pitch_angle: float32 [1], replicated, may hold values from -0.15 to 0.15
- near_tiles: int32 [2, 4, 4, 8], P('gx', 'gy', 'gz'), may hold values from -1 to 31, as said below
- send_rows: int32 [2, 4, 4, 8, 128], P('gx', 'gy', 'gz'), may hold values from -1 to 32767, as said below
- ghost_cell: int32 [2, 4, 4, 2048], P('gx', 'gy', 'gz'), may hold values from 0 to 32767, as said below
- ghost_src: int32 [2, 4, 4, 8, 2048], P('gx', 'gy', 'gz'), may hold values from 0 to 1023, as said below
- ghost_weight: float32 [2, 4, 4, 8, 2048], P('gx', 'gy', 'gz'), may hold values from 0 to 1, as said below
Outputs:
- new_velocity: float32 [3, 16, 128, 512], P(None, 'gx', 'gy', 'gz')
- new_nu_tilde: float32 [16, 128, 512], P('gx', 'gy', 'gz')
- wall_distance: float32 [16, 128, 512], P('gx', 'gy', 'gz')
The draws below stay inside these ranges and needn't reach their ends.
Inputs may be any that keep to these rules, and one draw needn't show every extreme that they name: `send_rows`: in each list of 128 slots from one device to one peer of gx+gz, live entries (local cell numbers of the sender) come first and the rest are -1. In every spanwise index some peer receives 128 live rows from every device. `ghost_src`: p * 128 + s names slot s of the rows that peer p sends to this device; it always names a live slot. `ghost_cell`: the 2048 entries of one device are distinct. `near_tiles`: distinct tiles first, the rest -1; some device lists 8 tiles. `ghost_weight`: the weights of one image point are non-negative and sum to one.
All inputs are finite; a program needn't handle non-finite values. No bound on the sum of `fluid_cells` on one device may be relied on, other than what follows from the above.
Results may differ from the reference program's by a relative error of at most 0.0003.
Values sent between devices are 32-bit elements; how exact they have to be, the bound alone decides.
A program may use at most 128 MiB of HBM per device.

```python
import math
import jax
import jax.numpy as jnp
from jax import lax

CX = 8
CY = 32
CZ = 128
TY = 8
STENCIL = 8
TRI_DEV = 128
CAP = 128
GHOSTS = 2048
NEAR_MAX = 8
NX = 16
NY = 128
NZ = 512
PEERS = 8
N_GX = 2
N_GY = 4
N_GZ = 4


def route_counts(key):
    base_key = jax.random.fold_in(key, 977)
    key_one, key_two = jax.random.split(base_key)
    peer_total = N_GX * N_GZ
    base_count = jax.random.randint(key_one, (N_GX, N_GY, N_GZ, peer_total), CAP // 2, CAP + 1)
    busiest = jax.random.randint(key_two, (N_GY,), 0, peer_total)
    target = jnp.arange(peer_total, dtype=jnp.int32)
    is_full = target[None, None, None, :] == busiest[None, :, None, None]
    return jnp.where(is_full, CAP, base_count).astype(jnp.int32)


def draw_send_rows(key, part):
    counts = route_counts(key)
    key = jax.random.fold_in(key, 3)
    chosen = jax.random.randint(key, (N_GX, N_GY, N_GZ, N_GX * N_GZ, CAP), 0, CX * CY * CZ)
    slot_index = jnp.arange(CAP, dtype=jnp.int32)
    return jnp.where(slot_index < counts[..., None], chosen, -1).astype(jnp.int32)


def draw_ghost_src(key, part):
    counts = route_counts(key)
    key = jax.random.fold_in(key, 5)
    key_one, key_two = jax.random.split(key)
    peer_total = N_GX * N_GZ
    full_shape = (N_GX, N_GY, N_GZ, STENCIL, GHOSTS)
    source = jax.random.randint(key_one, full_shape, 0, peer_total)
    count_table = counts.transpose(1, 0, 2, 3).reshape(N_GY, peer_total, peer_total)
    receiver = jnp.arange(N_GX, dtype=jnp.int32)[:, None] * N_GZ + jnp.arange(N_GZ, dtype=jnp.int32)[None, :]
    span_index = jnp.arange(N_GY, dtype=jnp.int32)
    slot_limit = count_table[span_index[None, :, None, None, None], source, receiver[:, None, :, None, None]]
    offset = jax.random.randint(key_two, full_shape, 0, slot_limit)
    return (source * CAP + offset).astype(jnp.int32)


def draw_ghost_cell(key, part):
    key = jax.random.fold_in(key, 7)
    key_list = jax.random.split(key, N_GX * N_GY * N_GZ)
    chosen = jax.vmap(lambda subkey: jax.random.permutation(subkey, CX * CY * CZ)[:GHOSTS])(key_list)
    return chosen.reshape(N_GX, N_GY, N_GZ, GHOSTS).astype(jnp.int32)


def draw_near_tiles(key, part):
    key = jax.random.fold_in(key, 11)
    key_one, key_two, key_three = jax.random.split(key, 3)
    devices = N_GX * N_GY * N_GZ
    tile_count = CX * (CY // TY)
    key_list = jax.random.split(key_one, devices)
    chosen = jax.vmap(lambda subkey: jax.random.permutation(subkey, tile_count)[:NEAR_MAX])(key_list)
    counts = jax.random.randint(key_two, (devices,), 1, NEAR_MAX + 1)
    fullest = jax.random.randint(key_three, (), 0, devices)
    counts = jnp.where(jnp.arange(devices, dtype=jnp.int32) == fullest, NEAR_MAX, counts)
    slot_index = jnp.arange(NEAR_MAX, dtype=jnp.int32)
    listed = jnp.where(slot_index[None, :] < counts[:, None], chosen, -1)
    return listed.reshape(N_GX, N_GY, N_GZ, NEAR_MAX).astype(jnp.int32)


def draw_surface(key, part):
    key = jax.random.fold_in(key, 13)
    unit_draw = jax.random.uniform(key, (N_GX, N_GZ, 3, TRI_DEV * N_GY), jnp.float32, -1.0, 1.0)
    extent = jnp.array([0.5 * CX, 0.5 * CY * N_GY, 0.5 * CZ], jnp.float32)
    return unit_draw * extent[None, None, :, None]


def draw_ghost_weight(key, part):
    key = jax.random.fold_in(key, 17)
    fraction = jax.random.uniform(key, (N_GX, N_GY, N_GZ, 3, GHOSTS), jnp.float32)
    corners = []
    for corner in range(8):
        weight = jnp.ones_like(fraction[:, :, :, 0])
        for direction in range(3):
            if corner >> direction & 1:
                weight = weight * fraction[:, :, :, direction]
            else:
                weight = weight * (1.0 - fraction[:, :, :, direction])
        corners.append(weight)
    return jnp.stack(corners, axis=3)


def with_ends(result, key, smallest, high):
    place = [jax.random.randint(jax.random.fold_in(key, axis), (), 0, length) for axis, length in enumerate(result.shape)]
    widest = result.shape.index(max(result.shape))
    beside = place[:widest] + [(place[widest] + 1) % result.shape[widest]] + place[widest + 1:]
    return result.at[tuple(place)].set(smallest).at[tuple(beside)].set(high)


def shard_levels(rng, shape, shards, low, largest):
    gain, own = 1.0, jax.random.fold_in(rng, 6)
    for position, blocks in shards:
        heights = jnp.exp(jax.random.uniform(jax.random.fold_in(own, position), (blocks,), jnp.float32, low / len(shards), largest / len(shards)))
        gain = gain * jnp.repeat(heights, shape[position] // blocks).reshape([-1 if axis == position else 1 for axis in range(len(shape))])
    return gain


def gaussian(rng, shape, deviation, bound, cuts=(), kind=jnp.bfloat16):
    result = jax.random.normal(rng, shape, jnp.float32) * deviation
    if len(cuts) > 0:
        result = shard_levels(rng, shape, cuts, -0.22, 0.18) * result
    return jnp.clip(result, min=-bound, max=bound).astype(kind)


def setup_inputs(seed: int = 0) -> dict:
    streams_of = jax.random.split(jax.random.key(seed), 11)
    velocity = gaussian(streams_of[0], (3, NX, NY, NZ), 1.0, 6.0, ((1, 2), (2, 4), (3, 4)), jnp.float32)
    nu_tilde = jnp.clip(jnp.exp(math.log(2.0) - 3.6888794 * jax.random.uniform(streams_of[1], (NX, NY, NZ), jnp.float32) ** shard_levels(streams_of[1], (NX, NY, NZ), ((0, 2), (1, 4), (2, 4)), -0.2, 0.2)), 0.05, 2.0)
    fluid_cells = with_ends((jax.random.randint(streams_of[2], (NX, NY, NZ), 0, 8) < 7).astype(jnp.int32), jax.random.fold_in(streams_of[2], 1), 0, 1)
    surface = draw_surface(jax.random.fold_in(streams_of[10], 71), 0)
    pitch_angle = jnp.clip(jax.random.uniform(streams_of[4], (1,), jnp.float32, -0.15, 0.15), -0.15, 0.15)
    near_tiles = draw_near_tiles(jax.random.fold_in(streams_of[10], 71), 0)
    send_rows = draw_send_rows(jax.random.fold_in(streams_of[10], 71), 0)
    ghost_cell = draw_ghost_cell(jax.random.fold_in(streams_of[10], 71), 0)
    ghost_src = draw_ghost_src(jax.random.fold_in(streams_of[10], 71), 0)
    ghost_weight = draw_ghost_weight(jax.random.fold_in(streams_of[10], 71), 0)
    return {"velocity": velocity, "nu_tilde": nu_tilde, "fluid_cells": fluid_cells, "surface": surface, "pitch_angle": pitch_angle, "near_tiles": near_tiles, "send_rows": send_rows, "ghost_cell": ghost_cell, "ghost_src": ghost_src, "ghost_weight": ghost_weight}


viscosity = 0.2
prod_coef = 0.1355
grad_coef = 0.622
sigma_inv = 1.5
karman = 0.41
visc_coef = 7.1
wall_coef = prod_coef / (karman * karman) + (1.0 + grad_coef) * sigma_inv
des_coef = 0.65
floor_rate = 0.3
dist_eps = 0.25
dist_cap = 8.0
time_step = 0.05

def to_blocks(fields):
    components = fields.shape[0]
    shaped = fields.reshape(components, N_GX, CX, N_GY, CY, N_GZ, CZ)
    shaped = shaped.transpose(1, 3, 5, 0, 2, 4, 6)
    return shaped.reshape(N_GX, N_GY, N_GZ, components, CX * CY * CZ)

def from_blocks(blocks):
    components = blocks.shape[3]
    shaped = blocks.reshape(N_GX, N_GY, N_GZ, components, CX, CY, CZ)
    shaped = shaped.transpose(3, 0, 4, 1, 5, 2, 6)
    return shaped.reshape(components, N_GX * CX, N_GY * CY, N_GZ * CZ)

def rotate(points, pitch_angle):
    cosine = jnp.cos(pitch_angle[0])
    sine_value = jnp.sin(pitch_angle[0])
    turned_x = cosine * points[0] + sine_value * points[2]
    turned_z = cosine * points[2] - sine_value * points[0]
    return jnp.stack([turned_x, points[1], turned_z])

def cell_coords(tile_list, y_offset, total_span, cells_x, cells_y, cells_z):
    per_row = cells_y // TY
    slots = tile_list.shape[0]
    safe_tiles = jnp.maximum(tile_list, 0)
    plane_index = (safe_tiles // per_row).astype(jnp.float32)
    band_row = safe_tiles % per_row * TY + y_offset
    row_index = band_row[:, None] + jnp.arange(TY, dtype=jnp.int32)[None, :]
    coord_x = jnp.broadcast_to((plane_index + 0.5 - 0.5 * cells_x)[:, None, None], (slots, TY, cells_z))
    coord_y = jnp.broadcast_to((row_index.astype(jnp.float32) + 0.5 - 0.5 * total_span)[:, :, None], (slots, TY, cells_z))
    depth = jnp.arange(cells_z, dtype=jnp.int32).astype(jnp.float32) + 0.5 - 0.5 * cells_z
    coord_z = jnp.broadcast_to(depth[None, None, :], (slots, TY, cells_z))
    return jnp.stack([coord_x, coord_y, coord_z]).reshape(3, slots, TY * cells_z)

def closest(cell_list, points, nearest_sq):

    def one_slot(slot_pair):
        slot_cells, best_now = slot_pair
        step_x = slot_cells[0][:, None] - points[0][None, :]
        step_y = slot_cells[1][:, None] - points[1][None, :]
        step_z = slot_cells[2][:, None] - points[2][None, :]
        squared = step_x * step_x + step_y * step_y + step_z * step_z
        return jnp.minimum(best_now, lax.optimization_barrier(jnp.min(squared, axis=1)))
    return lax.map(one_slot, (jnp.moveaxis(cell_list, 1, 0), nearest_sq))

def place_tiles(tile_list, values, cells_x, cells_y, cells_z):
    tile_count = cells_x * (cells_y // TY)
    tile_grid = jnp.full((tile_count, TY * cells_z), dist_cap, jnp.float32)
    target = jnp.where(tile_list >= 0, tile_list, tile_count)
    tile_grid = tile_grid.at[target].set(values, mode='drop')
    return tile_grid.reshape(cells_x, cells_y, cells_z)

def neighbour(padded, direction, offset, interior):
    slices = [slice(None)]
    for dimension in range(3):
        begin = 2 + (offset if dimension == direction else 0)
        slices.append(slice(begin, begin + interior[dimension]))
    return padded[tuple(slices)]

def advance(padded, wall_dist, fluid_cells):
    interior = (padded.shape[1] - 4, padded.shape[2] - 4, padded.shape[3] - 4)
    center = neighbour(padded, 0, 0, interior)
    gradient = []
    laplace = jnp.zeros_like(center)
    for direction in range(3):
        plus_one = neighbour(padded, direction, 1, interior)
        minus_one = neighbour(padded, direction, -1, interior)
        plus_two = neighbour(padded, direction, 2, interior)
        minus_two = neighbour(padded, direction, -2, interior)
        gradient.append((minus_two - plus_two + 8.0 * (plus_one - minus_one)) / 12.0)
        laplace = laplace + (plus_one + minus_one - 2.0 * center)
    moving = center[:3]
    working = center[3]
    curl_x = gradient[1][2] - gradient[2][1]
    curl_y = gradient[2][0] - gradient[0][2]
    curl_z = gradient[0][1] - gradient[1][0]
    vort_rate = jnp.maximum(jnp.sqrt(curl_x * curl_x + curl_y * curl_y + curl_z * curl_z), floor_rate)
    positive = jnp.maximum(working, 0.0)
    chi_ratio = positive / viscosity
    chi_cubed = chi_ratio * chi_ratio * chi_ratio
    eddy_visc = positive * chi_cubed / (chi_cubed + visc_coef ** 3)
    diffusion = viscosity + eddy_visc
    shield_arg = diffusion / (vort_rate * karman * karman * wall_dist * wall_dist)
    shield = 1.0 - jnp.tanh((8.0 * shield_arg) ** 3)
    length = wall_dist - shield * jnp.maximum(wall_dist - des_coef, 0.0)
    convect = moving[0] * gradient[0] + moving[1] * gradient[1] + moving[2] * gradient[2]
    grad_sq = gradient[0][3] * gradient[0][3] + gradient[1][3] * gradient[1][3] + gradient[2][3] * gradient[2][3]
    nu_rhs = -convect[3] + sigma_inv * ((viscosity + positive) * laplace[3] + grad_coef * grad_sq) + prod_coef * vort_rate * working - wall_coef * working * jnp.abs(working) / (length * length)
    vel_rhs = -convect[:3] + diffusion[None] * laplace[:3]
    fluid_mask = fluid_cells.astype(jnp.float32)
    new_velocity = moving + time_step * fluid_mask[None] * vel_rhs
    new_nu = working + time_step * fluid_mask * nu_rhs
    return (new_velocity, new_nu)

def fill_ghosts(fields, send_rows, ghost_src, ghost_weight, ghost_cell):
    blocks = to_blocks(fields)
    live_rows = send_rows >= 0
    safe_rows = jnp.where(live_rows, send_rows, 0)

    def pick(block_state, row_list, live_mask):
        return jnp.where(live_mask[None], block_state[:, row_list], 0.0)
    outgoing = jax.vmap(jax.vmap(jax.vmap(pick)))(blocks, safe_rows, live_rows)
    outgoing = outgoing.reshape(N_GX, N_GY, N_GZ, 4, N_GX, N_GZ, CAP)
    incoming = outgoing.transpose(4, 1, 5, 3, 0, 2, 6).reshape(N_GX, N_GY, N_GZ, 4, PEERS * CAP)

    def interpolate(block_state, buffer, sources, weights, cell_list):
        values = buffer[:, sources]
        ghost_value = -lax.optimization_barrier(jnp.sum(weights[None] * values, axis=1))
        return block_state.at[:, cell_list].set(ghost_value)
    filled = jax.vmap(jax.vmap(jax.vmap(interpolate)))(blocks, incoming, ghost_src, ghost_weight, ghost_cell)
    return from_blocks(filled)

def wall_field(surface, pitch_angle, near_tiles):

    def one_device(device_id):
        col_x = device_id // (N_GY * N_GZ)
        span_index = device_id // N_GZ % N_GY
        col_z = device_id % N_GZ
        points = rotate(surface[col_x, col_z], pitch_angle)
        tile_list = near_tiles[col_x, span_index, col_z]
        cell_list = cell_coords(tile_list, span_index * CY, NY, CX, CY, CZ)
        initial = jnp.full((tile_list.shape[0], TY * CZ), jnp.inf, jnp.float32)
        nearest_sq = closest(cell_list, points, initial)
        distance = jnp.minimum(jnp.sqrt(nearest_sq + dist_eps), dist_cap)
        return place_tiles(tile_list, distance, CX, CY, CZ).reshape(1, CX * CY * CZ)
    blocks = lax.map(one_device, jnp.arange(N_GX * N_GY * N_GZ, dtype=jnp.int32))
    return from_blocks(blocks.reshape(N_GX, N_GY, N_GZ, 1, CX * CY * CZ))[0]

def reference(velocity, nu_tilde, fluid_cells, surface, pitch_angle, near_tiles, send_rows, ghost_cell, ghost_src, ghost_weight):
    fields = jnp.concatenate([velocity, nu_tilde[None]], axis=0)
    filled = fill_ghosts(fields, send_rows, ghost_src, ghost_weight, ghost_cell)
    wall_distance = wall_field(surface, pitch_angle, near_tiles)
    padded = jnp.pad(filled, ((0, 0), (2, 2), (2, 2), (2, 2)))
    new_velocity, new_nu_tilde = advance(padded, wall_distance, fluid_cells)
    return (new_velocity, new_nu_tilde, wall_distance)
```

```python
import functools

import jax
import jax.numpy as jnp
from jax import lax
from jax.experimental import pallas as pl
from jax.experimental.pallas import tpu as pltpu
from jax.sharding import PartitionSpec as P

MESH = pl.DeviceIdType.MESH
TY = 8
LANES = 128

viscosity = 0.2
prod_coef = 0.1355
grad_coef = 0.622
sigma_inv = 1.5
karman = 0.41
visc_coef = 7.1
wall_coef = prod_coef / (karman * karman) + (1.0 + grad_coef) * sigma_inv
des_coef = 0.65
floor_rate = 0.3
dist_eps = 0.25
dist_cap = 8.0
time_step = 0.05


def lookup(row, lanes):
    table = jnp.broadcast_to(row, lanes.shape)
    return jnp.take_along_axis(table, lanes, axis=1, mode="promise_in_bounds")


def step_kernel(
    sizes,
    vel_ref,
    nu_ref,
    fluid_ref,
    surf_ref,
    pitch_ref,
    tiles_ref,
    rows_ref,
    cell_ref,
    src_ref,
    weight_ref,
    new_vel_ref,
    new_nu_ref,
    wall_ref,
    out_buf,
    in_buf,
    points,
    inverse,
    ghost,
    padded,
    edge_z,
    turn,
    pack_y,
    got_y,
    pack_z,
    got_z,
    flat_x,
    flat_y,
    flat_z2,
    dist,
    peer_send,
    peer_recv,
    point_send,
    point_recv,
    halo_send,
    halo_recv,
):
    nx, ny, nz = sizes
    peers = nx * nz
    _, cx, cy, cz = vel_ref.shape
    rows_y = cy // 8
    chunks = cell_ref.shape[1] // LANES
    a, b, c = (lax.axis_index(name) for name in ("gx", "gy", "gz"))
    me = a * nz + c
    slots = tiles_ref.shape[0]
    per_row = cy // TY
    lane = lax.broadcasted_iota(jnp.int32, (8, LANES), 1)

    def field(f, i, start, count):
        if f < 3:
            return vel_ref[f, i, pl.ds(start, count), :]
        return nu_ref[i, pl.ds(start, count), :]

    def peer_of(d):
        other = lax.rem(me + d, peers)
        return other, (lax.div(other, nz), b, lax.rem(other, nz))

    def column_of(d):
        other = lax.rem(b + d, ny)
        return other, (a, other, c)

    barrier = pltpu.get_barrier_semaphore()
    for d in range(1, peers):
        pl.semaphore_signal(barrier, inc=1, device_id=peer_of(d)[1], device_id_type=MESH)
    for d in range(1, ny):
        pl.semaphore_signal(barrier, inc=1, device_id=column_of(d)[1], device_id_type=MESH)

    angle = jnp.full((1, LANES), pitch_ref[0], jnp.float32)
    cosine, sine = jnp.cos(angle), jnp.sin(angle)
    px, py, pz = surf_ref[0:1, :], surf_ref[1:2, :], surf_ref[2:3, :]
    points[b] = jnp.concatenate(
        [cosine * px + sine * pz, py, cosine * pz - sine * px, jnp.zeros((5, LANES), jnp.float32)], axis=0
    )

    groups = peers // 8
    listed = [rows_ref[8 * g : 8 * g + 8, :] for g in range(groups)]
    listed_row = [lax.shift_right_arithmetic(x, 7) for x in listed]
    listed_lane = [x & (LANES - 1) for x in listed]

    def pick(i, acc):
        acc = list(acc)
        for j in range(cy):
            for g in range(groups):
                here = listed_row[g] == i * cy + j
                for f in range(4):
                    found = lookup(field(f, i, j, 1), listed_lane[g])
                    acc[4 * g + f] = jnp.where(here, found, acc[4 * g + f])
        return tuple(acc)

    picked = lax.fori_loop(0, cx, pick, tuple(jnp.zeros((8, LANES), jnp.float32) for _ in range(4 * groups)))
    for g in range(groups):
        for r in range(8):
            for f in range(4):
                out_buf[8 * g + r, f : f + 1, :] = picked[4 * g + f][r : r + 1, :]

    pl.semaphore_wait(barrier, peers - 1 + ny - 1)

    def peer_copy(d):
        other, device = peer_of(d)
        return pltpu.make_async_remote_copy(
            src_ref=out_buf.at[other],
            dst_ref=in_buf.at[me],
            send_sem=peer_send.at[d],
            recv_sem=peer_recv.at[d],
            device_id=device,
            device_id_type=MESH,
        )

    def point_copy(d):
        return pltpu.make_async_remote_copy(
            src_ref=points.at[b],
            dst_ref=points.at[b],
            send_sem=point_send.at[d],
            recv_sem=point_recv.at[d],
            device_id=column_of(d)[1],
            device_id_type=MESH,
        )

    peer_copies = [peer_copy(d) for d in range(1, peers)]
    for copy in peer_copies:
        copy.start()
    point_copies = [point_copy(d) for d in range(1, ny)]
    for copy in point_copies:
        copy.start()
    in_buf[me] = out_buf[me]

    def invert(pair, total):
        cells = cell_ref[:, pl.ds(pl.multiple_of(pair * 256, 256), 256)]
        at_row = lax.shift_right_arithmetic(cells, 7)
        at_lane = cells & (LANES - 1)
        row_id = lax.broadcasted_iota(jnp.int32, (cx * cy, 256), 0)
        lane_id = lax.broadcasted_iota(jnp.int32, (LANES, 256), 0)
        number = lax.broadcasted_iota(jnp.int32, (LANES, 256), 1) + pair * 256
        chunk_id = (lax.shift_right_arithmetic(number, 7) + 1).astype(jnp.float32)
        place = (number & (LANES - 1)).astype(jnp.float32)
        hit_row = jnp.where(row_id == at_row, 1.0, 0.0).astype(jnp.bfloat16)
        hit_lane = lane_id == at_lane
        code = jnp.concatenate(
            [jnp.where(hit_lane, chunk_id, 0.0), jnp.where(hit_lane, place, 0.0)], axis=0
        ).astype(jnp.bfloat16)
        return total + lax.dot_general(
            hit_row, code, (((1,), (1,)), ((), ())), preferred_element_type=jnp.float32
        )

    inverse[...] = lax.fori_loop(
        0, chunks // 2, invert, jnp.zeros((cx * cy, 2 * LANES), jnp.float32)
    ).astype(jnp.int32).reshape(cx, cy, 2 * LANES)

    for copy in peer_copies:
        copy.wait_recv()

    def interpolate(m, carry):
        at = pl.ds(pl.multiple_of(m * LANES, LANES), LANES)
        source = src_ref[:, at]
        weight = weight_ref[:, at]
        from_peer = lax.shift_right_arithmetic(source, 7)
        from_slot = source & (LANES - 1)

        def one_peer(p, acc):
            here = from_peer == p
            return tuple(
                jnp.where(here, lookup(in_buf[p, f : f + 1, :], from_slot), acc[f]) for f in range(4)
            )

        acc = tuple(jnp.zeros((8, LANES), jnp.float32) for _ in range(4))
        if peers <= 8:
            for p in range(peers):
                acc = one_peer(p, acc)
        else:
            acc = lax.fori_loop(0, peers, one_peer, acc)
        for f in range(4):
            ghost[f, pl.ds(m, 1), :] = -jnp.sum(weight * acc[f], axis=0, keepdims=True)
        return carry

    lax.fori_loop(0, chunks, interpolate, 0)

    def fill(i, carry):
        for jb in range(rows_y):
            chunk_id = inverse[i, 8 * jb : 8 * jb + 8, 0:LANES]
            place = inverse[i, 8 * jb : 8 * jb + 8, LANES : 2 * LANES]
            value = [field(f, i, 8 * jb, 8) for f in range(4)]
            for m in range(chunks):
                here = chunk_id == m + 1
                for f in range(4):
                    value[f] = jnp.where(here, lookup(ghost[f, m : m + 1, :], place), value[f])
            for f in range(4):
                padded[f, i + 2, 8 + 8 * jb : 16 + 8 * jb, :] = value[f]
        return carry

    low_high = ((a, nx), (b, ny), (c, nz))

    def exists(axis, side):
        index, count = low_high[axis]
        return index > 0 if side == 0 else index < count - 1

    def beside(axis, side):
        place = [a, b, c]
        place[axis] = place[axis] + (1 if side else -1)
        return tuple(place)

    def halo_copy(axis, side):
        if axis == 0:
            source = padded.at[:, 2:4, 8 : 8 + cy, :] if side == 0 else padded.at[:, cx : cx + 2, 8 : 8 + cy, :]
            target = padded.at[:, cx + 2 : cx + 4, 8 : 8 + cy, :] if side == 0 else padded.at[:, 0:2, 8 : 8 + cy, :]
        else:
            pack, got = ((pack_y, got_y), (pack_z, got_z))[axis - 1]
            source, target = pack.at[side], got.at[1 - side]
        return pltpu.make_async_remote_copy(
            src_ref=source,
            dst_ref=target,
            send_sem=halo_send.at[2 * axis + side],
            recv_sem=halo_recv.at[2 * axis + 1 - side],
            device_id=beside(axis, side),
            device_id_type=MESH,
        )

    def send_halo(axis):
        for side in range(2):
            @pl.when(exists(axis, side))
            def _():
                halo_copy(axis, side).start()

    def wait_halo(axis):
        for side in range(2):
            @pl.when(exists(axis, side))
            def _():
                pltpu.make_async_remote_copy(
                    src_ref=halo_source(axis, side),
                    dst_ref=halo_target(axis, side),
                    send_sem=halo_send.at[2 * axis + side],
                    recv_sem=halo_recv.at[2 * axis + side],
                    device_id=beside(axis, side),
                    device_id_type=MESH,
                ).wait_recv()

    def halo_source(axis, side):
        if axis == 0:
            return padded.at[:, 2:4, 8 : 8 + cy, :] if side == 0 else padded.at[:, cx : cx + 2, 8 : 8 + cy, :]
        return (pack_y, pack_z)[axis - 1].at[side]

    def halo_target(axis, side):
        if axis == 0:
            return padded.at[:, 0:2, 8 : 8 + cy, :] if side == 0 else padded.at[:, cx + 2 : cx + 4, 8 : 8 + cy, :]
        return (got_y, got_z)[axis - 1].at[side]

    lax.fori_loop(0, 2, fill, 0)
    lax.fori_loop(cx - 2, cx, fill, 0)
    send_halo(0)
    lax.fori_loop(2, cx - 2, fill, 0)
    for f in range(4):
        for i in range(cx):
            at = 2 * (f * cx + i)
            pack_y[0, at : at + 2, :] = padded[f, i + 2, 8:10, :]
            pack_y[1, at : at + 2, :] = padded[f, i + 2, 6 + cy : 8 + cy, :]
    send_halo(1)
    planes = LANES // cy
    blocks = cx // planes
    for f in range(4):
        for g in range(blocks):
            block = padded[f, 2 + planes * g : 2 + planes * (g + 1), 8 : 8 + cy, :].reshape(LANES, LANES)
            across = block.T
            at = 2 * (f * blocks + g)
            pack_z[0, at : at + 2, :] = across[0:2, :]
            pack_z[1, at : at + 2, :] = across[LANES - 2 : LANES, :]
    send_halo(2)

    for side in range(2):
        @pl.when(jnp.logical_not(exists(0, side)))
        def _():
            begin = 0 if side == 0 else cx + 2
            padded[:, begin : begin + 2, 8 : 8 + cy, :] = jnp.zeros((4, 2, cy, LANES), jnp.float32)

        @pl.when(jnp.logical_not(exists(1, side)))
        def _():
            got_y[side] = jnp.zeros(got_y.shape[1:], jnp.float32)

        @pl.when(jnp.logical_not(exists(2, side)))
        def _():
            got_z[side] = jnp.zeros(got_z.shape[1:], jnp.float32)

    for copy in point_copies:
        copy.wait_recv()
    deep = (lax.broadcasted_iota(jnp.int32, (LANES, LANES), 1).astype(jnp.float32) + 0.5) - 0.5 * cz
    for g in range(ny):
        at = slice(LANES * g, LANES * (g + 1))
        flat_x[at, :] = jnp.broadcast_to(points[g, 0:1, :], (LANES, LANES)).T
        flat_y[at, :] = jnp.broadcast_to(points[g, 1:2, :], (LANES, LANES)).T
        step_z = deep - jnp.broadcast_to(points[g, 2:3, :], (LANES, LANES)).T
        flat_z2[at, :] = step_z * step_z

    def one_slot(s, carry):
        tile = jnp.maximum(tiles_ref[s], 0)
        plane = lax.div(tile, per_row).astype(jnp.float32)
        first = lax.rem(tile, per_row) * TY + b * cy
        at_x = jnp.full((8, LANES), plane + 0.5 - 0.5 * cx, jnp.float32)
        at_y = [
            jnp.full((8, LANES), (first + r).astype(jnp.float32) + 0.5 - 0.5 * (ny * cy), jnp.float32)
            for r in range(TY)
        ]

        def some_points(k, best):
            for u in range(4):
                at = pl.ds(pl.multiple_of(k * 32, 32) + 8 * u, 8)
                step_x = at_x - flat_x[at, :]
                both = step_x * step_x + flat_z2[at, :]
                beside_y = flat_y[at, :]
                new = []
                for r in range(TY):
                    step_y = at_y[r] - beside_y
                    new.append(jnp.minimum(best[r], step_y * step_y + both))
                best = tuple(new)
            return best

        start = tuple(jnp.full((8, LANES), jnp.inf, jnp.float32) for _ in range(TY))
        best = lax.fori_loop(0, ny * LANES // 32, some_points, start)
        least = jnp.concatenate([jnp.min(x, axis=0, keepdims=True) for x in best], axis=0)
        dist[s] = jnp.minimum(jnp.sqrt(least + dist_eps), dist_cap)
        return carry

    lax.fori_loop(0, slots, one_slot, 0)

    for axis in range(3):
        wait_halo(axis)
    for f in range(4):
        for i in range(cx):
            at = 2 * (f * cx + i)
            padded[f, i + 2, 6:8, :] = got_y[0, at : at + 2, :]
            padded[f, i + 2, 8 + cy : 10 + cy, :] = got_y[1, at : at + 2, :]
    turn[...] = jnp.zeros(turn.shape, jnp.float32)
    for f in range(4):
        for g in range(blocks):
            at = 2 * (f * blocks + g)
            turn[0:2, :] = got_z[1, at : at + 2, :]
            turn[LANES - 2 : LANES, :] = got_z[0, at : at + 2, :]
            edge_z[f, planes * g : planes * (g + 1), :, :] = turn[...].T.reshape(planes, cy, LANES)

    def advance(i, carry):
        for jb in range(rows_y):
            advance_rows(i, jb)
        return carry

    def advance_rows(i, jb):
        center, gradient, laplace = [], [[], [], []], []

        def slope(m2, m1, p1, p2):
            return ((m2 - p2) + 8.0 * (p1 - m1)) * (1.0 / 12.0)

        for f in range(4):
            begin = 8 + 8 * jb
            mid = padded[f, i + 2, begin : begin + 8, :]
            x = [padded[f, i + 2 + h, begin : begin + 8, :] for h in (-2, -1, 1, 2)]
            y = [padded[f, i + 2, begin + h : begin + h + 8, :] for h in (-2, -1, 1, 2)]
            rim = edge_z[f, i, 8 * jb : 8 * jb + 8, :]
            z = [
                pltpu.roll(jnp.where(lane >= LANES - 2, rim, mid), 2, 1),
                pltpu.roll(jnp.where(lane >= LANES - 1, rim, mid), 1, 1),
                pltpu.roll(jnp.where(lane < 1, rim, mid), LANES - 1, 1),
                pltpu.roll(jnp.where(lane < 2, rim, mid), LANES - 2, 1),
            ]
            center.append(mid)
            for e, line in enumerate((x, y, z)):
                gradient[e].append(slope(*line))
            laplace.append(((x[1] + x[2]) + (y[1] + y[2])) + ((z[1] + z[2]) - 6.0 * mid))
        u, v, w, working = center
        curl_x = gradient[1][2] - gradient[2][1]
        curl_y = gradient[2][0] - gradient[0][2]
        curl_z = gradient[0][1] - gradient[1][0]
        rate = jnp.maximum(jnp.sqrt(curl_x * curl_x + curl_y * curl_y + curl_z * curl_z), floor_rate)
        positive = jnp.maximum(working, 0.0)
        chi = positive * (1.0 / viscosity)
        chi_cubed = chi * chi * chi
        diffusion = viscosity + positive * chi_cubed / (chi_cubed + visc_coef**3)
        wall = jnp.full((8, LANES), dist_cap, jnp.float32)
        number = i * per_row + jb
        for s in range(slots):
            wall = jnp.where(tiles_ref[s] == number, dist[s], wall)
        wall_ref[i, 8 * jb : 8 * jb + 8, :] = wall
        arg = (8.0 * diffusion) / (rate * (karman * karman) * (wall * wall))
        shield = 1.0 - jnp.tanh(arg * arg * arg)
        length = wall - shield * jnp.maximum(wall - des_coef, 0.0)
        scale = time_step * fluid_ref[i, 8 * jb : 8 * jb + 8, :].astype(jnp.float32)
        for f in range(4):
            convect = u * gradient[0][f] + v * gradient[1][f] + w * gradient[2][f]
            if f < 3:
                change = diffusion * laplace[f] - convect
                new_vel_ref[f, i, 8 * jb : 8 * jb + 8, :] = center[f] + scale * change
            else:
                squares = (
                    gradient[0][3] * gradient[0][3]
                    + gradient[1][3] * gradient[1][3]
                    + gradient[2][3] * gradient[2][3]
                )
                change = (
                    sigma_inv * ((viscosity + positive) * laplace[3] + grad_coef * squares)
                    - convect
                    + prod_coef * rate * working
                    - wall_coef * working * jnp.abs(working) / (length * length)
                )
                new_nu_ref[i, 8 * jb : 8 * jb + 8, :] = working + scale * change

    lax.fori_loop(0, cx, advance, 0)

    for copy in peer_copies + point_copies:
        copy.wait_send()
    for axis in range(3):
        for side in range(2):
            @pl.when(exists(axis, side))
            def _():
                halo_copy(axis, side).wait_send()


def on_device(
    velocity,
    nu_tilde,
    fluid_cells,
    surface,
    pitch_angle,
    near_tiles,
    send_rows,
    ghost_cell,
    ghost_src,
    ghost_weight,
):
    nx, ny, nz = (lax.axis_size(name) for name in ("gx", "gy", "gz"))
    peers = nx * nz
    _, cx, cy, cz = velocity.shape
    ghosts = ghost_cell.shape[-1]
    points_dev = surface.shape[-1]
    slots = near_tiles.shape[-1]
    vmem = pl.BlockSpec(memory_space=pltpu.VMEM)
    smem = pl.BlockSpec(memory_space=pltpu.SMEM)
    f32 = jnp.float32
    return pl.pallas_call(
        functools.partial(step_kernel, (nx, ny, nz)),
        out_shape=(
            jax.ShapeDtypeStruct(velocity.shape, f32),
            jax.ShapeDtypeStruct(nu_tilde.shape, f32),
            jax.ShapeDtypeStruct(nu_tilde.shape, f32),
        ),
        in_specs=[vmem, vmem, vmem, vmem, smem, smem, vmem, vmem, vmem, vmem],
        out_specs=(vmem, vmem, vmem),
        scratch_shapes=[
            pltpu.VMEM((peers, 4, LANES), f32),
            pltpu.VMEM((peers, 4, LANES), f32),
            pltpu.VMEM((ny, 8, points_dev), f32),
            pltpu.VMEM((cx, cy, 2 * LANES), jnp.int32),
            pltpu.VMEM((4, ghosts // LANES, LANES), f32),
            pltpu.VMEM((4, cx + 4, cy + 16, cz), f32),
            pltpu.VMEM((4, cx, cy, cz), f32),
            pltpu.VMEM((LANES, LANES), f32),
            pltpu.VMEM((2, 8 * cx, cz), f32),
            pltpu.VMEM((2, 8 * cx, cz), f32),
            pltpu.VMEM((2, 8 * cx * cy // LANES, LANES), f32),
            pltpu.VMEM((2, 8 * cx * cy // LANES, LANES), f32),
            pltpu.VMEM((ny * points_dev, cz), f32),
            pltpu.VMEM((ny * points_dev, cz), f32),
            pltpu.VMEM((ny * points_dev, cz), f32),
            pltpu.VMEM((slots, TY, cz), f32),
            pltpu.SemaphoreType.DMA((peers,)),
            pltpu.SemaphoreType.DMA((peers,)),
            pltpu.SemaphoreType.DMA((ny,)),
            pltpu.SemaphoreType.DMA((ny,)),
            pltpu.SemaphoreType.DMA((6,)),
            pltpu.SemaphoreType.DMA((6,)),
        ],
        compiler_params=pltpu.CompilerParams(
            collective_id=0, has_side_effects=True, vmem_limit_bytes=40 * 1024 * 1024
        ),
    )(
        velocity,
        nu_tilde,
        fluid_cells,
        surface[0, 0],
        pitch_angle,
        near_tiles[0, 0, 0],
        send_rows[0, 0, 0],
        ghost_cell[0, 0],
        ghost_src[0, 0, 0],
        ghost_weight[0, 0, 0],
    )


def solution(mesh):
    in_specs = (
        P(None, "gx", "gy", "gz"),
        P("gx", "gy", "gz"),
        P("gx", "gy", "gz"),
        P("gx", "gz", None, "gy"),
        P(),
        P("gx", "gy", "gz", None),
        P("gx", "gy", "gz", None, None),
        P("gx", "gy", "gz", None),
        P("gx", "gy", "gz", None, None),
        P("gx", "gy", "gz", None, None),
    )
    out_specs = (P(None, "gx", "gy", "gz"), P("gx", "gy", "gz"), P("gx", "gy", "gz"))
    return jax.shard_map(
        on_device, mesh=mesh, in_specs=in_specs, out_specs=out_specs, check_vma=False
    )
```

```python
import functools

import jax
import jax.numpy as jnp
from jax import lax
from jax.experimental import pallas as pl
from jax.experimental.pallas import tpu as pltpu
from jax.sharding import PartitionSpec as P

MESH = pl.DeviceIdType.MESH
TY = 8
LANES = 128

viscosity = 0.2
prod_coef = 0.1355
grad_coef = 0.622
sigma_inv = 1.5
karman = 0.41
visc_coef = 7.1
wall_coef = prod_coef / (karman * karman) + (1.0 + grad_coef) * sigma_inv
des_coef = 0.65
floor_rate = 0.3
dist_eps = 0.25
dist_cap = 8.0
time_step = 0.05


def lookup(row, lanes):
    table = jnp.broadcast_to(row, lanes.shape)
    return lax.gather(
        table,
        lanes[:, :, None],
        lax.GatherDimensionNumbers(
            offset_dims=(),
            collapsed_slice_dims=(1,),
            start_index_map=(1,),
            operand_batching_dims=(0,),
            start_indices_batching_dims=(0,),
        ),
        slice_sizes=(1, 1),
        mode=lax.GatherScatterMode.PROMISE_IN_BOUNDS,
    )


def step_kernel(
    sizes,
    vel_hbm,
    nu_hbm,
    fluid_hbm,
    surf_hbm,
    pitch_hbm,
    tiles_hbm,
    rows_hbm,
    cell_hbm,
    src_hbm,
    weight_hbm,
    new_vel,
    new_nu,
    wall_out,
    padded,
    edge_z,
    wall_ref,
    fluid_ref,
    vel_ref,
    nu_ref,
    fields,
    surf_ref,
    pitch_ref,
    tiles_ref,
    rows_ref,
    cell_ref,
    src_ref,
    weight_ref,
    out_buf,
    in_buf,
    points,
    inverse,
    ghost,
    turn,
    pack_y,
    got_y,
    pack_z,
    got_z,
    flat_x,
    flat_y,
    flat_z2,
    dist,
    tile_of,
    vel_sem,
    nu_sem,
    wall_sem,
    load,
    peer_send,
    peer_recv,
    point_send,
    point_recv,
    halo_send,
    halo_recv,
):
    pairs = (
        (rows_hbm, rows_ref),
        (vel_hbm, fields.at[0:3]),
        (nu_hbm, fields.at[3]),
        (pitch_hbm, pitch_ref),
        (surf_hbm, surf_ref),
        (cell_hbm, cell_ref),
        (src_hbm, src_ref),
        (weight_hbm, weight_ref),
        (tiles_hbm, tiles_ref),
        (fluid_hbm, fluid_ref),
    )
    loads = [pltpu.make_async_copy(x, y, load.at[i]) for i, (x, y) in enumerate(pairs)]
    for copy in loads:
        copy.start()

    nx, ny, nz = sizes
    peers = nx * nz
    _, cx, cy, cz = vel_hbm.shape
    rows_y = cy // 8
    chunks = cell_hbm.shape[1] // LANES
    a, b, c = (lax.axis_index(name) for name in ("gx", "gy", "gz"))
    me = a * nz + c
    lane = lax.broadcasted_iota(jnp.int32, (8, LANES), 1)
    slots = tiles_hbm.shape[1]
    per_row = cy // TY

    def field(f, i, start, count):
        return fields[f, i, pl.ds(start, count), :]

    def peer_of(d):
        other = lax.rem(me + d, peers)
        return other, (lax.div(other, nz), b, lax.rem(other, nz))

    def column_of(d):
        other = lax.rem(b + d, ny)
        return other, (a, other, c)

    barrier = pltpu.get_barrier_semaphore()
    for d in range(1, peers):
        pl.semaphore_signal(barrier, inc=1, device_id=peer_of(d)[1], device_id_type=MESH)
    for d in range(1, ny):
        pl.semaphore_signal(barrier, inc=1, device_id=column_of(d)[1], device_id_type=MESH)

    for copy in loads[0:5]:
        copy.wait()
    angle = jnp.full((1, LANES), pitch_ref[0], jnp.float32)
    cosine, sine = jnp.cos(angle), jnp.sin(angle)
    px, py, pz = surf_ref[0], surf_ref[1], surf_ref[2]
    points[b] = jnp.concatenate(
        [cosine * px + sine * pz, py, cosine * pz - sine * px, jnp.zeros((5, LANES), jnp.float32)], axis=0
    )

    groups = peers // 8
    listed = [rows_ref[8 * g : 8 * g + 8, :] for g in range(groups)]
    listed_row = [lax.shift_right_arithmetic(x, 7) for x in listed]
    listed_lane = [x & (LANES - 1) for x in listed]

    def pick(i, acc):
        acc = list(acc)
        for j in range(cy):
            for g in range(groups):
                here = listed_row[g] == i * cy + j
                for f in range(4):
                    found = lookup(field(f, i, j, 1), listed_lane[g])
                    acc[4 * g + f] = jnp.where(here, found, acc[4 * g + f])
        return tuple(acc)

    picked = lax.fori_loop(0, cx, pick, tuple(jnp.zeros((8, LANES), jnp.float32) for _ in range(4 * groups)))
    for g in range(groups):
        for r in range(8):
            for f in range(4):
                out_buf[8 * g + r, f : f + 1, :] = picked[4 * g + f][r : r + 1, :]

    pl.semaphore_wait(barrier, peers - 1 + ny - 1)

    def peer_copy(d):
        other, device = peer_of(d)
        return pltpu.make_async_remote_copy(
            src_ref=out_buf.at[other],
            dst_ref=in_buf.at[me],
            send_sem=peer_send.at[d],
            recv_sem=peer_recv.at[d],
            device_id=device,
            device_id_type=MESH,
        )

    def point_copy(d):
        return pltpu.make_async_remote_copy(
            src_ref=points.at[b],
            dst_ref=points.at[b],
            send_sem=point_send.at[d],
            recv_sem=point_recv.at[d],
            device_id=column_of(d)[1],
            device_id_type=MESH,
        )

    peer_copies = [peer_copy(d) for d in range(1, peers)]
    for copy in peer_copies:
        copy.start()
    point_copies = [point_copy(d) for d in range(1, ny)]
    for copy in point_copies:
        copy.start()
    in_buf[me] = out_buf[me]

    for copy in loads[5:]:
        copy.wait()

    def invert(pair, total):
        cells = cell_ref[:, pl.ds(pl.multiple_of(pair * 256, 256), 256)]
        at_row = lax.shift_right_arithmetic(cells, 7)
        at_lane = cells & (LANES - 1)
        row_id = lax.broadcasted_iota(jnp.int32, (cx * cy, 256), 0)
        lane_id = lax.broadcasted_iota(jnp.int32, (LANES, 256), 0)
        number = lax.broadcasted_iota(jnp.int32, (LANES, 256), 1) + pair * 256
        chunk_id = (lax.shift_right_arithmetic(number, 7) + 1).astype(jnp.float32)
        place = (number & (LANES - 1)).astype(jnp.float32)
        hit_row = jnp.where(row_id == at_row, 1.0, 0.0).astype(jnp.bfloat16)
        hit_lane = lane_id == at_lane
        code = jnp.concatenate(
            [jnp.where(hit_lane, chunk_id, 0.0), jnp.where(hit_lane, place, 0.0)], axis=0
        ).astype(jnp.bfloat16)
        return total + lax.dot_general(
            hit_row, code, (((1,), (1,)), ((), ())), preferred_element_type=jnp.float32
        )

    inverse[...] = lax.fori_loop(
        0, chunks // 2, invert, jnp.zeros((cx * cy, 2 * LANES), jnp.float32)
    ).astype(jnp.int32).reshape(cx, cy, 2 * LANES)

    for copy in peer_copies:
        copy.wait_recv()

    def interpolate(m, carry):
        at = pl.ds(pl.multiple_of(m * LANES, LANES), LANES)
        source = src_ref[:, at]
        weight = weight_ref[:, at]
        from_peer = lax.shift_right_arithmetic(source, 7)
        from_slot = source & (LANES - 1)

        def one_peer(p, acc):
            here = from_peer == p
            return tuple(
                jnp.where(here, lookup(in_buf[p, f : f + 1, :], from_slot), acc[f]) for f in range(4)
            )

        acc = tuple(jnp.zeros((8, LANES), jnp.float32) for _ in range(4))
        if peers <= 8:
            for p in range(peers):
                acc = one_peer(p, acc)
        else:
            acc = lax.fori_loop(0, peers, one_peer, acc)
        for f in range(4):
            ghost[f, pl.ds(m, 1), :] = -jnp.sum(weight * acc[f], axis=0, keepdims=True)
        return carry

    lax.fori_loop(0, chunks, interpolate, 0)

    def fill(i, carry):
        for jb in range(rows_y):
            chunk_id = inverse[i, 8 * jb : 8 * jb + 8, 0:LANES]
            place = inverse[i, 8 * jb : 8 * jb + 8, LANES : 2 * LANES]
            value = [field(f, i, 8 * jb, 8) for f in range(4)]
            for m in range(chunks):
                here = chunk_id == m + 1
                for f in range(4):
                    value[f] = jnp.where(here, lookup(ghost[f, m : m + 1, :], place), value[f])
            for f in range(4):
                padded[f, i + 2, 8 + 8 * jb : 16 + 8 * jb, :] = value[f]
        return carry

    low_high = ((a, nx), (b, ny), (c, nz))

    def exists(axis, side):
        index, count = low_high[axis]
        return index > 0 if side == 0 else index < count - 1

    def beside(axis, side):
        place = [a, b, c]
        place[axis] = place[axis] + (1 if side else -1)
        return tuple(place)

    def halo_copy(axis, side):
        if axis == 0:
            source = padded.at[:, 2:4, 8 : 8 + cy, :] if side == 0 else padded.at[:, cx : cx + 2, 8 : 8 + cy, :]
            target = padded.at[:, cx + 2 : cx + 4, 8 : 8 + cy, :] if side == 0 else padded.at[:, 0:2, 8 : 8 + cy, :]
        else:
            pack, got = ((pack_y, got_y), (pack_z, got_z))[axis - 1]
            source, target = pack.at[side], got.at[1 - side]
        return pltpu.make_async_remote_copy(
            src_ref=source,
            dst_ref=target,
            send_sem=halo_send.at[2 * axis + side],
            recv_sem=halo_recv.at[2 * axis + 1 - side],
            device_id=beside(axis, side),
            device_id_type=MESH,
        )

    def send_halo(axis):
        for side in range(2):
            @pl.when(exists(axis, side))
            def _():
                halo_copy(axis, side).start()

    def wait_halo(axis):
        for side in range(2):
            @pl.when(exists(axis, side))
            def _():
                pltpu.make_async_remote_copy(
                    src_ref=halo_source(axis, side),
                    dst_ref=halo_target(axis, side),
                    send_sem=halo_send.at[2 * axis + side],
                    recv_sem=halo_recv.at[2 * axis + side],
                    device_id=beside(axis, side),
                    device_id_type=MESH,
                ).wait_recv()

    def halo_source(axis, side):
        if axis == 0:
            return padded.at[:, 2:4, 8 : 8 + cy, :] if side == 0 else padded.at[:, cx : cx + 2, 8 : 8 + cy, :]
        return (pack_y, pack_z)[axis - 1].at[side]

    def halo_target(axis, side):
        if axis == 0:
            return padded.at[:, 0:2, 8 : 8 + cy, :] if side == 0 else padded.at[:, cx + 2 : cx + 4, 8 : 8 + cy, :]
        return (got_y, got_z)[axis - 1].at[side]

    lax.fori_loop(0, 2, fill, 0)
    lax.fori_loop(cx - 2, cx, fill, 0)
    send_halo(0)
    lax.fori_loop(2, cx - 2, fill, 0)
    for f in range(4):
        for i in range(cx):
            at = 2 * (f * cx + i)
            pack_y[0, at : at + 2, :] = padded[f, i + 2, 8:10, :]
            pack_y[1, at : at + 2, :] = padded[f, i + 2, 6 + cy : 8 + cy, :]
    send_halo(1)
    planes = LANES // cy
    blocks = cx // planes
    for f in range(4):
        for g in range(blocks):
            block = padded[f, 2 + planes * g : 2 + planes * (g + 1), 8 : 8 + cy, :].reshape(LANES, LANES)
            across = block.T
            at = 2 * (f * blocks + g)
            pack_z[0, at : at + 2, :] = across[0:2, :]
            pack_z[1, at : at + 2, :] = across[LANES - 2 : LANES, :]
    send_halo(2)

    for side in range(2):
        @pl.when(jnp.logical_not(exists(0, side)))
        def _():
            begin = 0 if side == 0 else cx + 2
            padded[:, begin : begin + 2, 8 : 8 + cy, :] = jnp.zeros((4, 2, cy, LANES), jnp.float32)

        @pl.when(jnp.logical_not(exists(1, side)))
        def _():
            got_y[side] = jnp.zeros(got_y.shape[1:], jnp.float32)

        @pl.when(jnp.logical_not(exists(2, side)))
        def _():
            got_z[side] = jnp.zeros(got_z.shape[1:], jnp.float32)

    for copy in point_copies:
        copy.wait_recv()
    deep = (lax.broadcasted_iota(jnp.int32, (LANES, LANES), 1).astype(jnp.float32) + 0.5) - 0.5 * cz
    for g in range(ny):
        at = slice(LANES * g, LANES * (g + 1))
        flat_x[at, :] = jnp.broadcast_to(points[g, 0:1, :], (LANES, LANES)).T
        flat_y[at, :] = jnp.broadcast_to(points[g, 1:2, :], (LANES, LANES)).T
        step_z = deep - jnp.broadcast_to(points[g, 2:3, :], (LANES, LANES)).T
        flat_z2[at, :] = step_z * step_z

    for s in range(slots):
        tile_of[s] = jnp.broadcast_to(tiles_ref[0:1, s : s + 1], (8, LANES))

    def one_slot(s, carry):
        tile = jnp.maximum(tile_of[s], 0)
        at_x = lax.div(tile, per_row).astype(jnp.float32) + (0.5 - 0.5 * cx)
        first = lax.rem(tile, per_row) * TY + b * cy
        at_y = first.astype(jnp.float32) + (0.5 - 0.5 * (ny * cy))

        def some_points(k, best):
            for u in range(4):
                at = pl.ds(pl.multiple_of(k * 32, 32) + 8 * u, 8)
                step_x = at_x - flat_x[at, :]
                step_y = at_y - flat_y[at, :]
                value = (step_x * step_x + step_y * step_y) + flat_z2[at, :]
                twice = step_y + step_y
                new = [jnp.minimum(best[0], value)]
                for r in range(1, TY):
                    value = value + twice
                    new.append(jnp.minimum(best[r], value))
                best = tuple(new)
            return best

        start = tuple(jnp.full((8, LANES), jnp.inf, jnp.float32) for _ in range(TY))
        best = lax.fori_loop(0, ny * LANES // 32, some_points, start)
        least = jnp.concatenate(
            [jnp.min(x, axis=0, keepdims=True) + float(r * r) for r, x in enumerate(best)], axis=0
        )
        dist[s] = jnp.minimum(jnp.sqrt(least + dist_eps), dist_cap)
        return carry

    lax.fori_loop(0, slots, one_slot, 0)

    def place(i, carry):
        for jb in range(rows_y):
            wall = jnp.full((8, LANES), dist_cap, jnp.float32)
            for s in range(slots):
                wall = jnp.where(tile_of[s] == i * per_row + jb, dist[s], wall)
            wall_ref[i, 8 * jb : 8 * jb + 8, :] = wall
        return carry

    lax.fori_loop(0, cx, place, 0)
    wall_copy = pltpu.make_async_copy(wall_ref, wall_out, wall_sem)
    wall_copy.start()

    for axis in range(3):
        wait_halo(axis)
    for f in range(4):
        for i in range(cx):
            at = 2 * (f * cx + i)
            padded[f, i + 2, 6:8, :] = got_y[0, at : at + 2, :]
            padded[f, i + 2, 8 + cy : 10 + cy, :] = got_y[1, at : at + 2, :]
    turn[...] = jnp.zeros(turn.shape, jnp.float32)
    for f in range(4):
        for g in range(blocks):
            at = 2 * (f * blocks + g)
            turn[0:2, :] = got_z[1, at : at + 2, :]
            turn[LANES - 2 : LANES, :] = got_z[0, at : at + 2, :]
            edge_z[f, planes * g : planes * (g + 1), :, :] = turn[...].T.reshape(planes, cy, LANES)

    def plane_copies(i):
        return (
            pltpu.make_async_copy(vel_ref.at[:, i], new_vel.at[:, i], vel_sem.at[i]),
            pltpu.make_async_copy(nu_ref.at[i], new_nu.at[i], nu_sem.at[i]),
        )

    def advance(i, carry):
        for jb in range(rows_y):
            advance_rows(i, jb)
        for copy in plane_copies(i):
            copy.start()
        return carry

    def advance_rows(i, jb):
        center, gradient, laplace = [], [[], [], []], []

        def slope(m2, m1, p1, p2):
            return ((m2 - p2) + 8.0 * (p1 - m1)) * (1.0 / 12.0)

        for f in range(4):
            begin = 8 + 8 * jb
            mid = padded[f, i + 2, begin : begin + 8, :]
            x = [padded[f, i + 2 + h, begin : begin + 8, :] for h in (-2, -1, 1, 2)]
            y = [padded[f, i + 2, begin + h : begin + h + 8, :] for h in (-2, -1, 1, 2)]
            rim = edge_z[f, i, 8 * jb : 8 * jb + 8, :]
            z = [
                pltpu.roll(jnp.where(lane >= LANES - 2, rim, mid), 2, 1),
                pltpu.roll(jnp.where(lane >= LANES - 1, rim, mid), 1, 1),
                pltpu.roll(jnp.where(lane < 1, rim, mid), LANES - 1, 1),
                pltpu.roll(jnp.where(lane < 2, rim, mid), LANES - 2, 1),
            ]
            center.append(mid)
            for e, line in enumerate((x, y, z)):
                gradient[e].append(slope(*line))
            laplace.append(((x[1] + x[2]) + (y[1] + y[2])) + ((z[1] + z[2]) - 6.0 * mid))
        u, v, w, working = center
        curl_x = gradient[1][2] - gradient[2][1]
        curl_y = gradient[2][0] - gradient[0][2]
        curl_z = gradient[0][1] - gradient[1][0]
        rate = jnp.maximum(jnp.sqrt(curl_x * curl_x + curl_y * curl_y + curl_z * curl_z), floor_rate)
        positive = jnp.maximum(working, 0.0)
        chi = positive * (1.0 / viscosity)
        chi_cubed = chi * chi * chi
        diffusion = viscosity + positive * chi_cubed / (chi_cubed + visc_coef**3)
        wall = wall_ref[i, 8 * jb : 8 * jb + 8, :]
        arg = (8.0 * diffusion) / (rate * (karman * karman) * (wall * wall))
        shield = 1.0 - jnp.tanh(arg * arg * arg)
        length = wall - shield * jnp.maximum(wall - des_coef, 0.0)
        scale = time_step * fluid_ref[i, 8 * jb : 8 * jb + 8, :].astype(jnp.float32)
        for f in range(4):
            convect = u * gradient[0][f] + v * gradient[1][f] + w * gradient[2][f]
            if f < 3:
                change = diffusion * laplace[f] - convect
                vel_ref[f, i, 8 * jb : 8 * jb + 8, :] = center[f] + scale * change
            else:
                squares = (
                    gradient[0][3] * gradient[0][3]
                    + gradient[1][3] * gradient[1][3]
                    + gradient[2][3] * gradient[2][3]
                )
                change = (
                    sigma_inv * ((viscosity + positive) * laplace[3] + grad_coef * squares)
                    - convect
                    + prod_coef * rate * working
                    - wall_coef * working * jnp.abs(working) / (length * length)
                )
                nu_ref[i, 8 * jb : 8 * jb + 8, :] = working + scale * change

    lax.fori_loop(0, cx, advance, 0)

    for copy in peer_copies + point_copies:
        copy.wait_send()
    for axis in range(3):
        for side in range(2):
            @pl.when(exists(axis, side))
            def _():
                halo_copy(axis, side).wait_send()

    def finish(i, carry):
        for copy in plane_copies(i):
            copy.wait()
        return carry

    lax.fori_loop(0, cx, finish, 0)
    wall_copy.wait()


def hand_over(vel, nu, wall, new_vel, new_nu, wall_out, sems):
    copies = [
        pltpu.make_async_copy(x, y, sems.at[i])
        for i, (x, y) in enumerate(((vel, new_vel), (nu, new_nu), (wall, wall_out)))
    ]
    for copy in copies:
        copy.start()
    for copy in copies:
        copy.wait()


def on_device(
    velocity,
    nu_tilde,
    fluid_cells,
    surface,
    pitch_angle,
    near_tiles,
    send_rows,
    ghost_cell,
    ghost_src,
    ghost_weight,
):
    nx, ny, nz = (lax.axis_size(name) for name in ("gx", "gy", "gz"))
    peers = nx * nz
    _, cx, cy, cz = velocity.shape
    ghosts = ghost_cell.shape[-1]
    points_dev = surface.shape[-1]
    slots = near_tiles.shape[-1]
    hbm = pl.BlockSpec(memory_space=pltpu.HBM)
    f32, i32 = jnp.float32, jnp.int32
    limit = 60 * 1024 * 1024
    results = (
        jax.ShapeDtypeStruct(velocity.shape, f32),
        jax.ShapeDtypeStruct(nu_tilde.shape, f32),
        jax.ShapeDtypeStruct(nu_tilde.shape, f32),
    )
    work = pl.pallas_call(
        functools.partial(step_kernel, (nx, ny, nz)),
        out_shape=results,
        in_specs=[hbm] * 10,
        out_specs=(hbm,) * 3,
        scratch_shapes=[
            pltpu.VMEM((4, cx + 4, cy + 16, cz), f32),
            pltpu.VMEM((4, cx, cy, cz), f32),
            pltpu.VMEM((cx, cy, cz), f32),
            pltpu.VMEM((cx, cy, cz), i32),
            pltpu.VMEM(velocity.shape, f32),
            pltpu.VMEM(nu_tilde.shape, f32),
            pltpu.VMEM((4, cx, cy, cz), f32),
            pltpu.VMEM((3, 1, points_dev), f32),
            pltpu.SMEM((1,), f32),
            pltpu.VMEM((1, slots), i32),
            pltpu.VMEM((peers, LANES), i32),
            pltpu.VMEM((1, ghosts), i32),
            pltpu.VMEM((8, ghosts), i32),
            pltpu.VMEM((8, ghosts), f32),
            pltpu.VMEM((peers, 4, LANES), f32),
            pltpu.VMEM((peers, 4, LANES), f32),
            pltpu.VMEM((ny, 8, points_dev), f32),
            pltpu.VMEM((cx, cy, 2 * LANES), i32),
            pltpu.VMEM((4, ghosts // LANES, LANES), f32),
            pltpu.VMEM((LANES, LANES), f32),
            pltpu.VMEM((2, 8 * cx, cz), f32),
            pltpu.VMEM((2, 8 * cx, cz), f32),
            pltpu.VMEM((2, 8 * cx * cy // LANES, LANES), f32),
            pltpu.VMEM((2, 8 * cx * cy // LANES, LANES), f32),
            pltpu.VMEM((ny * points_dev, cz), f32),
            pltpu.VMEM((ny * points_dev, cz), f32),
            pltpu.VMEM((ny * points_dev, cz), f32),
            pltpu.VMEM((slots, TY, cz), f32),
            pltpu.VMEM((slots, TY, cz), i32),
            pltpu.SemaphoreType.DMA((cx,)),
            pltpu.SemaphoreType.DMA((cx,)),
            pltpu.SemaphoreType.DMA,
            pltpu.SemaphoreType.DMA((10,)),
            pltpu.SemaphoreType.DMA((peers,)),
            pltpu.SemaphoreType.DMA((peers,)),
            pltpu.SemaphoreType.DMA((ny,)),
            pltpu.SemaphoreType.DMA((ny,)),
            pltpu.SemaphoreType.DMA((6,)),
            pltpu.SemaphoreType.DMA((6,)),
        ],
        compiler_params=pltpu.CompilerParams(
            collective_id=0, has_side_effects=True, vmem_limit_bytes=limit
        ),
    )(
        velocity,
        nu_tilde,
        fluid_cells,
        jnp.transpose(surface, (0, 2, 1, 3))[0],
        pitch_angle,
        near_tiles[0, 0],
        send_rows[0, 0, 0],
        ghost_cell[0, 0],
        ghost_src[0, 0, 0],
        ghost_weight[0, 0, 0],
    )
    return pl.pallas_call(
        hand_over,
        out_shape=results,
        in_specs=[hbm] * 3,
        out_specs=(hbm,) * 3,
        scratch_shapes=[pltpu.SemaphoreType.DMA((3,))],
        compiler_params=pltpu.CompilerParams(vmem_limit_bytes=limit),
    )(*work)


def solution(mesh):
    in_specs = (
        P(None, "gx", "gy", "gz"),
        P("gx", "gy", "gz"),
        P("gx", "gy", "gz"),
        P("gx", "gz", None, "gy"),
        P(),
        P("gx", "gy", "gz", None),
        P("gx", "gy", "gz", None, None),
        P("gx", "gy", "gz", None),
        P("gx", "gy", "gz", None, None),
        P("gx", "gy", "gz", None, None),
    )
    out_specs = (P(None, "gx", "gy", "gz"), P("gx", "gy", "gz"), P("gx", "gy", "gz"))
    return jax.shard_map(
        on_device, mesh=mesh, in_specs=in_specs, out_specs=out_specs, check_vma=False
    )
```

```python
import functools

import jax
import jax.numpy as jnp
from jax import lax
from jax.experimental import pallas as pl
from jax.experimental.pallas import tpu as pltpu
from jax.sharding import PartitionSpec as P

MESH = pl.DeviceIdType.MESH
TY = 8
LANES = 128

viscosity = 0.2
prod_coef = 0.1355
grad_coef = 0.622
sigma_inv = 1.5
karman = 0.41
visc_coef = 7.1
wall_coef = prod_coef / (karman * karman) + (1.0 + grad_coef) * sigma_inv
des_coef = 0.65
floor_rate = 0.3
dist_eps = 0.25
dist_cap = 8.0
time_step = 0.05


def lookup(row, lanes):
    table = jnp.broadcast_to(row, lanes.shape)
    return lax.gather(
        table,
        lanes[:, :, None],
        lax.GatherDimensionNumbers(
            offset_dims=(),
            collapsed_slice_dims=(1,),
            start_index_map=(1,),
            operand_batching_dims=(0,),
            start_indices_batching_dims=(0,),
        ),
        slice_sizes=(1, 1),
        mode=lax.GatherScatterMode.PROMISE_IN_BOUNDS,
    )


def step_kernel(
    sizes,
    vel_hbm,
    nu_hbm,
    fluid_hbm,
    surf_hbm,
    pitch_hbm,
    tiles_hbm,
    rows_hbm,
    cell_hbm,
    src_hbm,
    weight_hbm,
    new_vel,
    new_nu,
    wall_out,
    padded,
    edge_z,
    wall_ref,
    fluid_ref,
    vel_ref,
    nu_ref,
    fields,
    surf_ref,
    pitch_ref,
    tiles_ref,
    rows_ref,
    cell_ref,
    src_ref,
    weight_ref,
    out_buf,
    in_buf,
    points,
    inverse,
    ghost,
    turn,
    by_row,
    by_lane,
    pack_y,
    got_y,
    pack_z,
    got_z,
    flat_x,
    flat_y,
    flat_z2,
    dist,
    tile_of,
    vel_sem,
    nu_sem,
    wall_sem,
    load,
    peer_send,
    peer_recv,
    point_send,
    point_recv,
    halo_send,
    halo_recv,
):
    pairs = (
        (pitch_hbm, pitch_ref),
        (surf_hbm, surf_ref),
        (rows_hbm, rows_ref),
        (vel_hbm, fields.at[0:3]),
        (nu_hbm, fields.at[3]),
        (cell_hbm, cell_ref),
        (src_hbm, src_ref),
        (weight_hbm, weight_ref),
        (tiles_hbm, tiles_ref),
        (fluid_hbm, fluid_ref),
    )
    loads = [pltpu.make_async_copy(x, y, load.at[i]) for i, (x, y) in enumerate(pairs)]
    for copy in loads:
        copy.start()

    nx, ny, nz = sizes
    peers = nx * nz
    _, cx, cy, cz = vel_hbm.shape
    rows_y = cy // 8
    chunks = cell_hbm.shape[1] // LANES
    a, b, c = (lax.axis_index(name) for name in ("gx", "gy", "gz"))
    me = a * nz + c
    lane = lax.broadcasted_iota(jnp.int32, (8, LANES), 1)
    slots = tiles_hbm.shape[1]
    per_row = cy // TY

    def field(f, i, start, count):
        return fields[f, i, pl.ds(start, count), :]

    def peer_of(d):
        other = lax.rem(me + d, peers)
        return other, (lax.div(other, nz), b, lax.rem(other, nz))

    def column_of(d):
        other = lax.rem(b + d, ny)
        return other, (a, other, c)

    barrier = pltpu.get_barrier_semaphore()
    for d in range(1, peers):
        pl.semaphore_signal(barrier, inc=1, device_id=peer_of(d)[1], device_id_type=MESH)
    for d in range(1, ny):
        pl.semaphore_signal(barrier, inc=1, device_id=column_of(d)[1], device_id_type=MESH)

    for copy in loads[0:2]:
        copy.wait()
    angle = jnp.full((1, LANES), pitch_ref[0], jnp.float32)
    cosine, sine = jnp.cos(angle), jnp.sin(angle)
    px, py, pz = surf_ref[0], surf_ref[1], surf_ref[2]
    points[b] = jnp.concatenate(
        [cosine * px + sine * pz, py, cosine * pz - sine * px, jnp.zeros((5, LANES), jnp.float32)], axis=0
    )

    turn[...] = jnp.zeros(turn.shape, jnp.float32)
    pl.semaphore_wait(barrier, peers - 1 + ny - 1)

    def point_copy(d):
        return pltpu.make_async_remote_copy(
            src_ref=points.at[b],
            dst_ref=points.at[b],
            send_sem=point_send.at[d],
            recv_sem=point_recv.at[d],
            device_id=column_of(d)[1],
            device_id_type=MESH,
        )

    point_copies = [point_copy(d) for d in range(1, ny)]
    for copy in point_copies:
        copy.start()

    for copy in loads[2:5]:
        copy.wait()
    groups = peers // 8
    listed = [rows_ref[8 * g : 8 * g + 8, :] for g in range(groups)]
    listed_row = [lax.shift_right_arithmetic(x, 7) for x in listed]
    listed_lane = [x & (LANES - 1) for x in listed]

    def pick(i, acc):
        acc = list(acc)
        for j in range(cy):
            for g in range(groups):
                here = listed_row[g] == i * cy + j
                for f in range(4):
                    found = lookup(field(f, i, j, 1), listed_lane[g])
                    acc[4 * g + f] = jnp.where(here, found, acc[4 * g + f])
        return tuple(acc)

    picked = lax.fori_loop(0, cx, pick, tuple(jnp.zeros((8, LANES), jnp.float32) for _ in range(4 * groups)))
    for g in range(groups):
        for r in range(8):
            for f in range(4):
                out_buf[8 * g + r, f : f + 1, :] = picked[4 * g + f][r : r + 1, :]

    def peer_copy(d):
        other, device = peer_of(d)
        return pltpu.make_async_remote_copy(
            src_ref=out_buf.at[other],
            dst_ref=in_buf.at[me],
            send_sem=peer_send.at[d],
            recv_sem=peer_recv.at[d],
            device_id=device,
            device_id_type=MESH,
        )

    peer_copies = [peer_copy(d) for d in range(1, peers)]
    for copy in peer_copies:
        copy.start()
    in_buf[me] = out_buf[me]

    for copy in loads[5:]:
        copy.wait()

    for copy in point_copies:
        copy.wait_recv()
    deep = (lax.broadcasted_iota(jnp.int32, (LANES, LANES), 1).astype(jnp.float32) + 0.5) - 0.5 * cz
    for g in range(ny):
        at = slice(LANES * g, LANES * (g + 1))
        flat_x[at, :] = jnp.broadcast_to(points[g, 0:1, :], (LANES, LANES)).T
        flat_y[at, :] = jnp.broadcast_to(points[g, 1:2, :], (LANES, LANES)).T
        step_z = deep - jnp.broadcast_to(points[g, 2:3, :], (LANES, LANES)).T
        flat_z2[at, :] = step_z * step_z

    for s in range(slots):
        tile_of[s] = jnp.broadcast_to(tiles_ref[0:1, s : s + 1], (8, LANES))

    def one_slot(s, carry):
        tile = jnp.maximum(tile_of[s], 0)
        at_x = lax.div(tile, per_row).astype(jnp.float32) + (0.5 - 0.5 * cx)
        first = lax.rem(tile, per_row) * TY + b * cy
        at_y = first.astype(jnp.float32) + (0.5 - 0.5 * (ny * cy))

        def some_points(k, best):
            for u in range(16):
                at = pl.ds(pl.multiple_of(k * LANES, LANES) + 8 * u, 8)
                step_x = at_x - flat_x[at, :]
                step_y = at_y - flat_y[at, :]
                value = (step_x * step_x + step_y * step_y) + flat_z2[at, :]
                twice = step_y + step_y
                new = [jnp.minimum(best[0], value)]
                for r in range(1, TY):
                    value = value + twice
                    new.append(jnp.minimum(best[r], value))
                best = tuple(new)
            return best

        start = tuple(jnp.full((8, LANES), jnp.inf, jnp.float32) for _ in range(TY))
        best = lax.fori_loop(0, ny, some_points, start)
        least = jnp.concatenate(
            [jnp.min(x, axis=0, keepdims=True) + float(r * r) for r, x in enumerate(best)], axis=0
        )
        dist[s] = jnp.minimum(jnp.sqrt(least + dist_eps), dist_cap)
        return carry

    ghosts = cell_ref.shape[1]
    cells = cell_ref[...]
    number = lax.broadcasted_iota(jnp.int32, (1, ghosts), 1)
    chunk_id = (lax.shift_right_arithmetic(number, 7) + 1).astype(jnp.float32)
    in_chunk = (number & (LANES - 1)).astype(jnp.float32)
    row_id = lax.broadcasted_iota(jnp.int32, (cx * cy, ghosts), 0)
    lane_id = lax.broadcasted_iota(jnp.int32, (LANES, ghosts), 0)
    hit_row = jnp.where(row_id == lax.shift_right_arithmetic(cells, 7), 1.0, 0.0)
    hit_lane = lane_id == (cells & (LANES - 1))
    by_row[...] = hit_row.astype(jnp.bfloat16)
    by_lane[0:LANES, :] = jnp.where(hit_lane, chunk_id, 0.0).astype(jnp.bfloat16)
    by_lane[LANES : 2 * LANES, :] = jnp.where(hit_lane, in_chunk, 0.0).astype(jnp.bfloat16)
    inverse[...] = (
        lax.dot_general(
            by_row[...], by_lane[...], (((1,), (1,)), ((), ())), preferred_element_type=jnp.float32
        )
        .astype(jnp.int32)
        .reshape(cx, cy, 2 * LANES)
    )

    lax.fori_loop(0, slots // 2, one_slot, 0)

    for copy in peer_copies:
        copy.wait_recv()

    def interpolate(m, carry):
        at = pl.ds(pl.multiple_of(m * LANES, LANES), LANES)
        source = src_ref[:, at]
        weight = weight_ref[:, at]
        from_peer = lax.shift_right_arithmetic(source, 7)
        from_slot = source & (LANES - 1)

        def one_peer(p, acc):
            here = from_peer == p
            return tuple(
                jnp.where(here, lookup(in_buf[p, f : f + 1, :], from_slot), acc[f]) for f in range(4)
            )

        acc = tuple(jnp.zeros((8, LANES), jnp.float32) for _ in range(4))
        if peers <= 8:
            for p in range(peers):
                acc = one_peer(p, acc)
        else:
            acc = lax.fori_loop(0, peers, one_peer, acc)
        for f in range(4):
            ghost[f, pl.ds(m, 1), :] = -jnp.sum(weight * acc[f], axis=0, keepdims=True)
        return carry

    lax.fori_loop(0, chunks, interpolate, 0, unroll=4 if peers <= 8 else 1)

    def fill(i, carry):
        for jb in range(rows_y):
            chunk_id = inverse[i, 8 * jb : 8 * jb + 8, 0:LANES]
            place = inverse[i, 8 * jb : 8 * jb + 8, LANES : 2 * LANES]
            value = [field(f, i, 8 * jb, 8) for f in range(4)]
            for m in range(chunks):
                here = chunk_id == m + 1
                for f in range(4):
                    value[f] = jnp.where(here, lookup(ghost[f, m : m + 1, :], place), value[f])
            for f in range(4):
                padded[f, i + 2, 8 + 8 * jb : 16 + 8 * jb, :] = value[f]
        return carry

    low_high = ((a, nx), (b, ny), (c, nz))

    def exists(axis, side):
        index, count = low_high[axis]
        return index > 0 if side == 0 else index < count - 1

    def beside(axis, side):
        place = [a, b, c]
        place[axis] = place[axis] + (1 if side else -1)
        return tuple(place)

    def halo_copy(axis, side):
        if axis == 0:
            source = padded.at[:, 2:4, 8 : 8 + cy, :] if side == 0 else padded.at[:, cx : cx + 2, 8 : 8 + cy, :]
            target = padded.at[:, cx + 2 : cx + 4, 8 : 8 + cy, :] if side == 0 else padded.at[:, 0:2, 8 : 8 + cy, :]
        else:
            pack, got = ((pack_y, got_y), (pack_z, got_z))[axis - 1]
            source, target = pack.at[side], got.at[1 - side]
        return pltpu.make_async_remote_copy(
            src_ref=source,
            dst_ref=target,
            send_sem=halo_send.at[2 * axis + side],
            recv_sem=halo_recv.at[2 * axis + 1 - side],
            device_id=beside(axis, side),
            device_id_type=MESH,
        )

    def send_halo(axis):
        for side in range(2):
            @pl.when(exists(axis, side))
            def _():
                halo_copy(axis, side).start()

    def wait_halo(axis):
        for side in range(2):
            @pl.when(exists(axis, side))
            def _():
                pltpu.make_async_remote_copy(
                    src_ref=halo_source(axis, side),
                    dst_ref=halo_target(axis, side),
                    send_sem=halo_send.at[2 * axis + side],
                    recv_sem=halo_recv.at[2 * axis + side],
                    device_id=beside(axis, side),
                    device_id_type=MESH,
                ).wait_recv()

    def halo_source(axis, side):
        if axis == 0:
            return padded.at[:, 2:4, 8 : 8 + cy, :] if side == 0 else padded.at[:, cx : cx + 2, 8 : 8 + cy, :]
        return (pack_y, pack_z)[axis - 1].at[side]

    def halo_target(axis, side):
        if axis == 0:
            return padded.at[:, 0:2, 8 : 8 + cy, :] if side == 0 else padded.at[:, cx + 2 : cx + 4, 8 : 8 + cy, :]
        return (got_y, got_z)[axis - 1].at[side]

    lax.fori_loop(0, 2, fill, 0)
    lax.fori_loop(cx - 2, cx, fill, 0)
    send_halo(0)
    lax.fori_loop(2, cx - 2, fill, 0)
    for f in range(4):
        for i in range(cx):
            at = 2 * (f * cx + i)
            pack_y[0, at : at + 2, :] = padded[f, i + 2, 8:10, :]
            pack_y[1, at : at + 2, :] = padded[f, i + 2, 6 + cy : 8 + cy, :]
    send_halo(1)
    planes = LANES // cy
    blocks = cx // planes
    for f in range(4):
        for g in range(blocks):
            block = padded[f, 2 + planes * g : 2 + planes * (g + 1), 8 : 8 + cy, :].reshape(LANES, LANES)
            across = block.T
            at = 2 * (f * blocks + g)
            pack_z[0, at : at + 2, :] = across[0:2, :]
            pack_z[1, at : at + 2, :] = across[LANES - 2 : LANES, :]
    send_halo(2)

    for side in range(2):
        @pl.when(jnp.logical_not(exists(0, side)))
        def _():
            begin = 0 if side == 0 else cx + 2
            padded[:, begin : begin + 2, 8 : 8 + cy, :] = jnp.zeros((4, 2, cy, LANES), jnp.float32)

        @pl.when(jnp.logical_not(exists(1, side)))
        def _():
            got_y[side] = jnp.zeros(got_y.shape[1:], jnp.float32)

        @pl.when(jnp.logical_not(exists(2, side)))
        def _():
            got_z[side] = jnp.zeros(got_z.shape[1:], jnp.float32)

    lax.fori_loop(slots // 2, slots, one_slot, 0)

    def place(i, carry):
        for jb in range(rows_y):
            wall = jnp.full((8, LANES), dist_cap, jnp.float32)
            for s in range(slots):
                wall = jnp.where(tile_of[s] == i * per_row + jb, dist[s], wall)
            wall_ref[i, 8 * jb : 8 * jb + 8, :] = wall
        return carry

    lax.fori_loop(0, cx, place, 0)
    wall_copy = pltpu.make_async_copy(wall_ref, wall_out, wall_sem)
    wall_copy.start()

    for axis in range(3):
        wait_halo(axis)
    for f in range(4):
        for i in range(cx):
            at = 2 * (f * cx + i)
            padded[f, i + 2, 6:8, :] = got_y[0, at : at + 2, :]
            padded[f, i + 2, 8 + cy : 10 + cy, :] = got_y[1, at : at + 2, :]
    for f in range(4):
        for g in range(blocks):
            at = 2 * (f * blocks + g)
            turn[f * blocks + g, 0:2, :] = got_z[1, at : at + 2, :]
            turn[f * blocks + g, LANES - 2 : LANES, :] = got_z[0, at : at + 2, :]
            edge_z[f, planes * g : planes * (g + 1), :, :] = turn[f * blocks + g].T.reshape(planes, cy, LANES)

    def plane_copies(i):
        return (
            pltpu.make_async_copy(vel_ref.at[:, i], new_vel.at[:, i], vel_sem.at[i]),
            pltpu.make_async_copy(nu_ref.at[i], new_nu.at[i], nu_sem.at[i]),
        )

    def advance(i, carry):
        for jb in range(rows_y):
            advance_rows(i, jb)
        for copy in plane_copies(i):
            copy.start()
        return carry

    def advance_rows(i, jb):
        center, gradient, laplace = [], [[], [], []], []

        def slope(m2, m1, p1, p2):
            return ((m2 - p2) + 8.0 * (p1 - m1)) * (1.0 / 12.0)

        for f in range(4):
            begin = 8 + 8 * jb
            mid = padded[f, i + 2, begin : begin + 8, :]
            x = [padded[f, i + 2 + h, begin : begin + 8, :] for h in (-2, -1, 1, 2)]
            y = [padded[f, i + 2, begin + h : begin + h + 8, :] for h in (-2, -1, 1, 2)]
            rim = edge_z[f, i, 8 * jb : 8 * jb + 8, :]
            z = [
                pltpu.roll(jnp.where(lane >= LANES - 2, rim, mid), 2, 1),
                pltpu.roll(jnp.where(lane >= LANES - 1, rim, mid), 1, 1),
                pltpu.roll(jnp.where(lane < 1, rim, mid), LANES - 1, 1),
                pltpu.roll(jnp.where(lane < 2, rim, mid), LANES - 2, 1),
            ]
            center.append(mid)
            for e, line in enumerate((x, y, z)):
                gradient[e].append(slope(*line))
            laplace.append(((x[1] + x[2]) + (y[1] + y[2])) + ((z[1] + z[2]) - 6.0 * mid))
        u, v, w, working = center
        curl_x = gradient[1][2] - gradient[2][1]
        curl_y = gradient[2][0] - gradient[0][2]
        curl_z = gradient[0][1] - gradient[1][0]
        rate = jnp.maximum(jnp.sqrt(curl_x * curl_x + curl_y * curl_y + curl_z * curl_z), floor_rate)
        positive = jnp.maximum(working, 0.0)
        chi = positive * (1.0 / viscosity)
        chi_cubed = chi * chi * chi
        diffusion = viscosity + positive * chi_cubed / (chi_cubed + visc_coef**3)
        wall = wall_ref[i, 8 * jb : 8 * jb + 8, :]
        arg = (8.0 * diffusion) / (rate * (karman * karman) * (wall * wall))
        shield = 1.0 - jnp.tanh(arg * arg * arg)
        length = wall - shield * jnp.maximum(wall - des_coef, 0.0)
        scale = time_step * fluid_ref[i, 8 * jb : 8 * jb + 8, :].astype(jnp.float32)
        for f in range(4):
            convect = u * gradient[0][f] + v * gradient[1][f] + w * gradient[2][f]
            if f < 3:
                change = diffusion * laplace[f] - convect
                vel_ref[f, i, 8 * jb : 8 * jb + 8, :] = center[f] + scale * change
            else:
                squares = (
                    gradient[0][3] * gradient[0][3]
                    + gradient[1][3] * gradient[1][3]
                    + gradient[2][3] * gradient[2][3]
                )
                change = (
                    sigma_inv * ((viscosity + positive) * laplace[3] + grad_coef * squares)
                    - convect
                    + prod_coef * rate * working
                    - wall_coef * working * jnp.abs(working) / (length * length)
                )
                nu_ref[i, 8 * jb : 8 * jb + 8, :] = working + scale * change

    lax.fori_loop(0, cx, advance, 0)

    for copy in peer_copies + point_copies:
        copy.wait_send()
    for axis in range(3):
        for side in range(2):
            @pl.when(exists(axis, side))
            def _():
                halo_copy(axis, side).wait_send()

    def finish(i, carry):
        for copy in plane_copies(i):
            copy.wait()
        return carry

    lax.fori_loop(0, cx, finish, 0)
    wall_copy.wait()


def hand_over(vel, nu, wall, new_vel, new_nu, wall_out, held, come, go):
    pieces = [(vel.at[f], new_vel.at[f]) for f in range(3)] + [(nu, new_nu), (wall, wall_out)]
    ins = [pltpu.make_async_copy(x, held.at[i], come.at[i]) for i, (x, _) in enumerate(pieces)]
    outs = [pltpu.make_async_copy(held.at[i], y, go.at[i]) for i, (_, y) in enumerate(pieces)]
    for copy in ins:
        copy.start()
    for first, second in zip(ins, outs):
        first.wait()
        second.start()
    for copy in outs:
        copy.wait()


def on_device(
    velocity,
    nu_tilde,
    fluid_cells,
    surface,
    pitch_angle,
    near_tiles,
    send_rows,
    ghost_cell,
    ghost_src,
    ghost_weight,
):
    nx, ny, nz = (lax.axis_size(name) for name in ("gx", "gy", "gz"))
    peers = nx * nz
    _, cx, cy, cz = velocity.shape
    ghosts = ghost_cell.shape[-1]
    points_dev = surface.shape[-1]
    slots = near_tiles.shape[-1]
    hbm = pl.BlockSpec(memory_space=pltpu.HBM)
    f32, i32 = jnp.float32, jnp.int32
    limit = 60 * 1024 * 1024
    results = (
        jax.ShapeDtypeStruct(velocity.shape, f32),
        jax.ShapeDtypeStruct(nu_tilde.shape, f32),
        jax.ShapeDtypeStruct(nu_tilde.shape, f32),
    )
    work = pl.pallas_call(
        functools.partial(step_kernel, (nx, ny, nz)),
        out_shape=results,
        in_specs=[hbm] * 10,
        out_specs=(hbm,) * 3,
        scratch_shapes=[
            pltpu.VMEM((4, cx + 4, cy + 16, cz), f32),
            pltpu.VMEM((4, cx, cy, cz), f32),
            pltpu.VMEM((cx, cy, cz), f32),
            pltpu.VMEM((cx, cy, cz), i32),
            pltpu.VMEM(velocity.shape, f32),
            pltpu.VMEM(nu_tilde.shape, f32),
            pltpu.VMEM((4, cx, cy, cz), f32),
            pltpu.VMEM((3, 1, points_dev), f32),
            pltpu.SMEM((1,), f32),
            pltpu.VMEM((1, slots), i32),
            pltpu.VMEM((peers, LANES), i32),
            pltpu.VMEM((1, ghosts), i32),
            pltpu.VMEM((8, ghosts), i32),
            pltpu.VMEM((8, ghosts), f32),
            pltpu.VMEM((peers, 4, LANES), f32),
            pltpu.VMEM((peers, 4, LANES), f32),
            pltpu.VMEM((ny, 8, points_dev), f32),
            pltpu.VMEM((cx, cy, 2 * LANES), i32),
            pltpu.VMEM((4, ghosts // LANES, LANES), f32),
            pltpu.VMEM((4 * cx * cy // LANES, LANES, LANES), f32),
            pltpu.VMEM((cx * cy, ghosts), jnp.bfloat16),
            pltpu.VMEM((2 * LANES, ghosts), jnp.bfloat16),
            pltpu.VMEM((2, 8 * cx, cz), f32),
            pltpu.VMEM((2, 8 * cx, cz), f32),
            pltpu.VMEM((2, 8 * cx * cy // LANES, LANES), f32),
            pltpu.VMEM((2, 8 * cx * cy // LANES, LANES), f32),
            pltpu.VMEM((ny * points_dev, cz), f32),
            pltpu.VMEM((ny * points_dev, cz), f32),
            pltpu.VMEM((ny * points_dev, cz), f32),
            pltpu.VMEM((slots, TY, cz), f32),
            pltpu.VMEM((slots, TY, cz), i32),
            pltpu.SemaphoreType.DMA((cx,)),
            pltpu.SemaphoreType.DMA((cx,)),
            pltpu.SemaphoreType.DMA,
            pltpu.SemaphoreType.DMA((10,)),
            pltpu.SemaphoreType.DMA((peers,)),
            pltpu.SemaphoreType.DMA((peers,)),
            pltpu.SemaphoreType.DMA((ny,)),
            pltpu.SemaphoreType.DMA((ny,)),
            pltpu.SemaphoreType.DMA((6,)),
            pltpu.SemaphoreType.DMA((6,)),
        ],
        compiler_params=pltpu.CompilerParams(
            collective_id=0, has_side_effects=True, vmem_limit_bytes=limit
        ),
    )(
        velocity,
        nu_tilde,
        fluid_cells,
        jnp.transpose(surface, (0, 2, 1, 3))[0],
        pitch_angle,
        near_tiles[0, 0],
        send_rows[0, 0, 0],
        ghost_cell[0, 0],
        ghost_src[0, 0, 0],
        ghost_weight[0, 0, 0],
    )
    return pl.pallas_call(
        hand_over,
        out_shape=results,
        in_specs=[hbm] * 3,
        out_specs=(hbm,) * 3,
        scratch_shapes=[
            pltpu.VMEM((5, cx, cy, cz), f32),
            pltpu.SemaphoreType.DMA((5,)),
            pltpu.SemaphoreType.DMA((5,)),
        ],
        compiler_params=pltpu.CompilerParams(vmem_limit_bytes=limit),
    )(*work)


def solution(mesh):
    in_specs = (
        P(None, "gx", "gy", "gz"),
        P("gx", "gy", "gz"),
        P("gx", "gy", "gz"),
        P("gx", "gz", None, "gy"),
        P(),
        P("gx", "gy", "gz", None),
        P("gx", "gy", "gz", None, None),
        P("gx", "gy", "gz", None),
        P("gx", "gy", "gz", None, None),
        P("gx", "gy", "gz", None, None),
    )
    out_specs = (P(None, "gx", "gy", "gz"), P("gx", "gy", "gz"), P("gx", "gy", "gz"))
    return jax.shard_map(
        on_device, mesh=mesh, in_specs=in_specs, out_specs=out_specs, check_vma=False
    )
```

```python
import functools

import jax
import jax.numpy as jnp
from jax import lax
from jax.experimental import pallas as pl
from jax.experimental.pallas import tpu as pltpu
from jax.sharding import PartitionSpec as P

MESH = pl.DeviceIdType.MESH
TY = 8
LANES = 128

viscosity = 0.2
prod_coef = 0.1355
grad_coef = 0.622
sigma_inv = 1.5
karman = 0.41
visc_coef = 7.1
wall_coef = prod_coef / (karman * karman) + (1.0 + grad_coef) * sigma_inv
des_coef = 0.65
floor_rate = 0.3
dist_eps = 0.25
dist_cap = 8.0
time_step = 0.05


def lookup(row, lanes):
    table = jnp.broadcast_to(row, lanes.shape)
    return lax.gather(
        table,
        lanes[:, :, None],
        lax.GatherDimensionNumbers(
            offset_dims=(),
            collapsed_slice_dims=(1,),
            start_index_map=(1,),
            operand_batching_dims=(0,),
            start_indices_batching_dims=(0,),
        ),
        slice_sizes=(1, 1),
        mode=lax.GatherScatterMode.PROMISE_IN_BOUNDS,
    )


def step_kernel(
    sizes,
    vel_hbm,
    nu_hbm,
    fluid_hbm,
    surf_hbm,
    pitch_hbm,
    tiles_hbm,
    rows_hbm,
    cell_hbm,
    src_hbm,
    weight_hbm,
    new_vel,
    new_nu,
    wall_out,
    padded,
    edge_z,
    wall_ref,
    fluid_ref,
    vel_ref,
    nu_ref,
    fields,
    surf_ref,
    pitch_ref,
    tiles_ref,
    rows_ref,
    cell_ref,
    src_ref,
    weight_ref,
    out_buf,
    in_buf,
    points,
    is_ghost,
    spread,
    choose,
    parts,
    turn,
    by_row,
    by_lane,
    pack_y,
    got_y,
    pack_z,
    got_z,
    flat_x,
    flat_y,
    flat_z2,
    dist,
    tile_of,
    vel_sem,
    nu_sem,
    wall_sem,
    load,
    peer_send,
    peer_recv,
    point_send,
    point_recv,
    halo_send,
    halo_recv,
):
    pairs = (
        (pitch_hbm, pitch_ref),
        (surf_hbm, surf_ref),
        (rows_hbm, rows_ref),
        (vel_hbm, fields.at[0:3]),
        (nu_hbm, fields.at[3]),
        (cell_hbm, cell_ref),
        (src_hbm, src_ref),
        (weight_hbm, weight_ref),
        (tiles_hbm, tiles_ref),
        (fluid_hbm, fluid_ref),
    )
    loads = [pltpu.make_async_copy(x, y, load.at[i]) for i, (x, y) in enumerate(pairs)]
    for copy in loads:
        copy.start()

    nx, ny, nz = sizes
    peers = nx * nz
    _, cx, cy, cz = vel_hbm.shape
    rows_y = cy // 8
    chunks = cell_hbm.shape[1] // LANES
    a, b, c = (lax.axis_index(name) for name in ("gx", "gy", "gz"))
    me = a * nz + c
    lane = lax.broadcasted_iota(jnp.int32, (8, LANES), 1)
    slots = tiles_hbm.shape[1]
    per_row = cy // TY

    def peer_of(d):
        other = lax.rem(me + d, peers)
        return other, (lax.div(other, nz), b, lax.rem(other, nz))

    def column_of(d):
        other = lax.rem(b + d, ny)
        return other, (a, other, c)

    barrier = pltpu.get_barrier_semaphore()
    for d in range(1, peers):
        pl.semaphore_signal(barrier, inc=1, device_id=peer_of(d)[1], device_id_type=MESH)
    for d in range(1, ny):
        pl.semaphore_signal(barrier, inc=1, device_id=column_of(d)[1], device_id_type=MESH)

    for copy in loads[0:2]:
        copy.wait()
    angle = jnp.full((1, LANES), pitch_ref[0], jnp.float32)
    cosine, sine = jnp.cos(angle), jnp.sin(angle)
    px, py, pz = surf_ref[0], surf_ref[1], surf_ref[2]
    points[b] = jnp.concatenate(
        [cosine * px + sine * pz, py, cosine * pz - sine * px, jnp.zeros((5, LANES), jnp.float32)], axis=0
    )

    turn[...] = jnp.zeros(turn.shape, jnp.float32)
    pl.semaphore_wait(barrier, peers - 1 + ny - 1)

    def point_copy(d):
        return pltpu.make_async_remote_copy(
            src_ref=points.at[b],
            dst_ref=points.at[b],
            send_sem=point_send.at[d],
            recv_sem=point_recv.at[d],
            device_id=column_of(d)[1],
            device_id_type=MESH,
        )

    point_copies = [point_copy(d) for d in range(1, ny)]
    for copy in point_copies:
        copy.start()

    cells_hi = cx * cy
    loads[2].wait()
    row_number = lax.broadcasted_iota(jnp.int32, (cells_hi, LANES), 0)
    lane_number = lax.broadcasted_iota(jnp.int32, (LANES, 2 * LANES), 0)
    for p in range(peers):
        wanted = lax.shift_right_arithmetic(rows_ref[p : p + 1, :], 7)
        hit = jnp.where(row_number == wanted, 1.0, 0.0).astype(jnp.bfloat16)
        choose[0:cells_hi, LANES * p : LANES * (p + 1)] = hit
        choose[cells_hi : 2 * cells_hi, LANES * p : LANES * (p + 1)] = hit

    for copy in loads[3:5]:
        copy.wait()
    for f in range(4):
        across = fields[f].reshape(cells_hi, LANES).T
        big = across.astype(jnp.bfloat16)
        rest = (across - big.astype(jnp.float32)).astype(jnp.bfloat16)
        parts[LANES * f : LANES * (f + 1), 0:cells_hi] = big
        parts[LANES * f : LANES * (f + 1), cells_hi : 2 * cells_hi] = rest

    def pick(k, carry):
        at = pl.multiple_of(k * 2 * LANES, 2 * LANES)
        found = jnp.dot(
            parts[...], choose[:, pl.ds(at, 2 * LANES)], preferred_element_type=jnp.float32
        )
        both = jnp.concatenate([rows_ref[pl.ds(2 * k, 1), :], rows_ref[pl.ds(2 * k + 1, 1), :]], axis=1)
        here = lane_number == (both & (LANES - 1))
        for f in range(4):
            row = jnp.sum(
                jnp.where(here, found[LANES * f : LANES * (f + 1), :], 0.0), axis=0, keepdims=True
            )
            out_buf[2 * k, f : f + 1, :] = row[:, 0:LANES]
            out_buf[2 * k + 1, f : f + 1, :] = row[:, LANES : 2 * LANES]
        return carry

    lax.fori_loop(0, peers // 2, pick, 0, unroll=peers <= 8)

    def peer_copy(d):
        other, device = peer_of(d)
        return pltpu.make_async_remote_copy(
            src_ref=out_buf.at[other],
            dst_ref=in_buf.at[me],
            send_sem=peer_send.at[d],
            recv_sem=peer_recv.at[d],
            device_id=device,
            device_id_type=MESH,
        )

    peer_copies = [peer_copy(d) for d in range(1, peers)]
    for copy in peer_copies:
        copy.start()
    in_buf[me] = out_buf[me]

    for copy in loads[5:]:
        copy.wait()

    for copy in point_copies:
        copy.wait_recv()
    deep = (lax.broadcasted_iota(jnp.int32, (LANES, LANES), 1).astype(jnp.float32) + 0.5) - 0.5 * cz
    for g in range(ny):
        at = slice(LANES * g, LANES * (g + 1))
        flat_x[at, :] = jnp.broadcast_to(points[g, 0:1, :], (LANES, LANES)).T
        flat_y[at, :] = jnp.broadcast_to(points[g, 1:2, :], (LANES, LANES)).T
        step_z = deep - jnp.broadcast_to(points[g, 2:3, :], (LANES, LANES)).T
        flat_z2[at, :] = step_z * step_z

    for s in range(slots):
        tile_of[s] = jnp.broadcast_to(tiles_ref[0:1, s : s + 1], (8, LANES))

    def one_slot(s, carry):
        tile = jnp.maximum(tile_of[s], 0)
        at_x = lax.div(tile, per_row).astype(jnp.float32) + (0.5 - 0.5 * cx)
        first = lax.rem(tile, per_row) * TY + b * cy
        at_y = first.astype(jnp.float32) + (0.5 - 0.5 * (ny * cy))

        def some_points(k, best):
            for u in range(16):
                at = pl.ds(pl.multiple_of(k * LANES, LANES) + 8 * u, 8)
                step_x = at_x - flat_x[at, :]
                step_y = at_y - flat_y[at, :]
                value = (step_x * step_x + step_y * step_y) + flat_z2[at, :]
                twice = step_y + step_y
                new = [jnp.minimum(best[0], value)]
                for r in range(1, TY):
                    value = value + twice
                    new.append(jnp.minimum(best[r], value))
                best = tuple(new)
            return best

        start = tuple(jnp.full((8, LANES), jnp.inf, jnp.float32) for _ in range(TY))
        best = lax.fori_loop(0, ny, some_points, start)
        least = jnp.concatenate(
            [jnp.min(x, axis=0, keepdims=True) + float(r * r) for r, x in enumerate(best)], axis=0
        )
        dist[s] = jnp.minimum(jnp.sqrt(least + dist_eps), dist_cap)
        return carry

    ghosts = cell_ref.shape[1]
    cells = cell_ref[...]
    row_id = lax.broadcasted_iota(jnp.int32, (cells_hi, ghosts), 0)
    lane_id = lax.broadcasted_iota(jnp.int32, (LANES, ghosts), 0)
    hit_row = jnp.where(row_id == lax.shift_right_arithmetic(cells, 7), 1.0, 0.0).astype(jnp.bfloat16)
    by_row[:, 0:ghosts] = hit_row
    by_row[:, ghosts : 2 * ghosts] = hit_row
    by_lane[...] = jnp.where(lane_id == (cells & (LANES - 1)), 1.0, 0.0).astype(jnp.bfloat16)
    last_dims = (((1,), (1,)), ((), ()))
    is_ghost[...] = lax.dot_general(
        by_row[:, 0:ghosts], by_lane[...], last_dims, preferred_element_type=jnp.float32
    ).reshape(cx, cy, LANES)

    lax.fori_loop(0, slots // 2, one_slot, 0)

    for copy in peer_copies:
        copy.wait_recv()

    def interpolate(m, carry):
        at = pl.ds(pl.multiple_of(m * LANES, LANES), LANES)
        source = src_ref[:, at]
        weight = weight_ref[:, at]
        from_peer = lax.shift_right_arithmetic(source, 7)
        from_slot = source & (LANES - 1)

        def one_peer(p, acc):
            here = from_peer == p
            return tuple(
                jnp.where(here, lookup(in_buf[p, f : f + 1, :], from_slot), acc[f]) for f in range(4)
            )

        acc = tuple(jnp.zeros((8, LANES), jnp.float32) for _ in range(4))
        if peers <= 8:
            for p in range(peers):
                acc = one_peer(p, acc)
        else:
            acc = lax.fori_loop(0, peers, one_peer, acc)
        for f in range(4):
            value = -jnp.sum(weight * acc[f], axis=0, keepdims=True)
            big = value.astype(jnp.bfloat16)
            rest = (value - big.astype(jnp.float32)).astype(jnp.bfloat16)
            hit = by_lane[:, at]
            to = pl.ds(pl.multiple_of(ghosts + m * LANES, LANES), LANES)
            spread[LANES * f : LANES * (f + 1), at] = hit * jnp.broadcast_to(big, hit.shape)
            spread[LANES * f : LANES * (f + 1), to] = hit * jnp.broadcast_to(rest, hit.shape)
        return carry

    lax.fori_loop(0, chunks, interpolate, 0, unroll=4 if peers <= 8 else 1)

    stored = lax.dot_general(by_row[...], spread[...], last_dims, preferred_element_type=jnp.float32)
    for f in range(4):
        value = stored[:, LANES * f : LANES * (f + 1)].reshape(cx, cy, LANES)
        padded[f, 2 : cx + 2, 8 : 8 + cy, :] = jnp.where(is_ghost[...] > 0.5, value, fields[f])

    low_high = ((a, nx), (b, ny), (c, nz))

    def exists(axis, side):
        index, count = low_high[axis]
        return index > 0 if side == 0 else index < count - 1

    def beside(axis, side):
        place = [a, b, c]
        place[axis] = place[axis] + (1 if side else -1)
        return tuple(place)

    def halo_copy(axis, side):
        if axis == 0:
            source = padded.at[:, 2:4, 8 : 8 + cy, :] if side == 0 else padded.at[:, cx : cx + 2, 8 : 8 + cy, :]
            target = padded.at[:, cx + 2 : cx + 4, 8 : 8 + cy, :] if side == 0 else padded.at[:, 0:2, 8 : 8 + cy, :]
        else:
            pack, got = ((pack_y, got_y), (pack_z, got_z))[axis - 1]
            source, target = pack.at[side], got.at[1 - side]
        return pltpu.make_async_remote_copy(
            src_ref=source,
            dst_ref=target,
            send_sem=halo_send.at[2 * axis + side],
            recv_sem=halo_recv.at[2 * axis + 1 - side],
            device_id=beside(axis, side),
            device_id_type=MESH,
        )

    def send_halo(axis):
        for side in range(2):
            @pl.when(exists(axis, side))
            def _():
                halo_copy(axis, side).start()

    def wait_halo(axis):
        for side in range(2):
            @pl.when(exists(axis, side))
            def _():
                pltpu.make_async_remote_copy(
                    src_ref=halo_source(axis, side),
                    dst_ref=halo_target(axis, side),
                    send_sem=halo_send.at[2 * axis + side],
                    recv_sem=halo_recv.at[2 * axis + side],
                    device_id=beside(axis, side),
                    device_id_type=MESH,
                ).wait_recv()

    def halo_source(axis, side):
        if axis == 0:
            return padded.at[:, 2:4, 8 : 8 + cy, :] if side == 0 else padded.at[:, cx : cx + 2, 8 : 8 + cy, :]
        return (pack_y, pack_z)[axis - 1].at[side]

    def halo_target(axis, side):
        if axis == 0:
            return padded.at[:, 0:2, 8 : 8 + cy, :] if side == 0 else padded.at[:, cx + 2 : cx + 4, 8 : 8 + cy, :]
        return (got_y, got_z)[axis - 1].at[side]

    send_halo(0)
    for f in range(4):
        for i in range(cx):
            at = 2 * (f * cx + i)
            pack_y[0, at : at + 2, :] = padded[f, i + 2, 8:10, :]
            pack_y[1, at : at + 2, :] = padded[f, i + 2, 6 + cy : 8 + cy, :]
    send_halo(1)
    planes = LANES // cy
    blocks = cx // planes
    for f in range(4):
        for g in range(blocks):
            block = padded[f, 2 + planes * g : 2 + planes * (g + 1), 8 : 8 + cy, :].reshape(LANES, LANES)
            across = block.T
            at = 2 * (f * blocks + g)
            pack_z[0, at : at + 2, :] = across[0:2, :]
            pack_z[1, at : at + 2, :] = across[LANES - 2 : LANES, :]
    send_halo(2)

    for side in range(2):
        @pl.when(jnp.logical_not(exists(0, side)))
        def _():
            begin = 0 if side == 0 else cx + 2
            padded[:, begin : begin + 2, 8 : 8 + cy, :] = jnp.zeros((4, 2, cy, LANES), jnp.float32)

        @pl.when(jnp.logical_not(exists(1, side)))
        def _():
            got_y[side] = jnp.zeros(got_y.shape[1:], jnp.float32)

        @pl.when(jnp.logical_not(exists(2, side)))
        def _():
            got_z[side] = jnp.zeros(got_z.shape[1:], jnp.float32)

    lax.fori_loop(slots // 2, slots, one_slot, 0)

    def place(i, carry):
        for jb in range(rows_y):
            wall = jnp.full((8, LANES), dist_cap, jnp.float32)
            for s in range(slots):
                wall = jnp.where(tile_of[s] == i * per_row + jb, dist[s], wall)
            wall_ref[i, 8 * jb : 8 * jb + 8, :] = wall
        return carry

    lax.fori_loop(0, cx, place, 0)
    wall_copy = pltpu.make_async_copy(wall_ref, wall_out, wall_sem)
    wall_copy.start()

    for axis in range(3):
        wait_halo(axis)
    for f in range(4):
        for i in range(cx):
            at = 2 * (f * cx + i)
            padded[f, i + 2, 6:8, :] = got_y[0, at : at + 2, :]
            padded[f, i + 2, 8 + cy : 10 + cy, :] = got_y[1, at : at + 2, :]
    for f in range(4):
        for g in range(blocks):
            at = 2 * (f * blocks + g)
            turn[f * blocks + g, 0:2, :] = got_z[1, at : at + 2, :]
            turn[f * blocks + g, LANES - 2 : LANES, :] = got_z[0, at : at + 2, :]
            edge_z[f, planes * g : planes * (g + 1), :, :] = turn[f * blocks + g].T.reshape(planes, cy, LANES)

    def plane_copies(i):
        return (
            pltpu.make_async_copy(vel_ref.at[:, i], new_vel.at[:, i], vel_sem.at[i]),
            pltpu.make_async_copy(nu_ref.at[i], new_nu.at[i], nu_sem.at[i]),
        )

    def advance(i, carry):
        for jb in range(rows_y):
            advance_rows(i, jb)
        for copy in plane_copies(i):
            copy.start()
        return carry

    def advance_rows(i, jb):
        center, gradient, laplace = [], [[], [], []], []

        def slope(m2, m1, p1, p2):
            return ((m2 - p2) + 8.0 * (p1 - m1)) * (1.0 / 12.0)

        for f in range(4):
            begin = 8 + 8 * jb
            mid = padded[f, i + 2, begin : begin + 8, :]
            x = [padded[f, i + 2 + h, begin : begin + 8, :] for h in (-2, -1, 1, 2)]
            y = [padded[f, i + 2, begin + h : begin + h + 8, :] for h in (-2, -1, 1, 2)]
            rim = edge_z[f, i, 8 * jb : 8 * jb + 8, :]
            z = [
                pltpu.roll(jnp.where(lane >= LANES - 2, rim, mid), 2, 1),
                pltpu.roll(jnp.where(lane >= LANES - 1, rim, mid), 1, 1),
                pltpu.roll(jnp.where(lane < 1, rim, mid), LANES - 1, 1),
                pltpu.roll(jnp.where(lane < 2, rim, mid), LANES - 2, 1),
            ]
            center.append(mid)
            for e, line in enumerate((x, y, z)):
                gradient[e].append(slope(*line))
            laplace.append(((x[1] + x[2]) + (y[1] + y[2])) + ((z[1] + z[2]) - 6.0 * mid))
        u, v, w, working = center
        curl_x = gradient[1][2] - gradient[2][1]
        curl_y = gradient[2][0] - gradient[0][2]
        curl_z = gradient[0][1] - gradient[1][0]
        rate = jnp.maximum(jnp.sqrt(curl_x * curl_x + curl_y * curl_y + curl_z * curl_z), floor_rate)
        positive = jnp.maximum(working, 0.0)
        chi = positive * (1.0 / viscosity)
        chi_cubed = chi * chi * chi
        diffusion = viscosity + positive * chi_cubed / (chi_cubed + visc_coef**3)
        wall = wall_ref[i, 8 * jb : 8 * jb + 8, :]
        arg = (8.0 * diffusion) / (rate * (karman * karman) * (wall * wall))
        shield = 1.0 - jnp.tanh(arg * arg * arg)
        length = wall - shield * jnp.maximum(wall - des_coef, 0.0)
        scale = time_step * fluid_ref[i, 8 * jb : 8 * jb + 8, :].astype(jnp.float32)
        for f in range(4):
            convect = u * gradient[0][f] + v * gradient[1][f] + w * gradient[2][f]
            if f < 3:
                change = diffusion * laplace[f] - convect
                vel_ref[f, i, 8 * jb : 8 * jb + 8, :] = center[f] + scale * change
            else:
                squares = (
                    gradient[0][3] * gradient[0][3]
                    + gradient[1][3] * gradient[1][3]
                    + gradient[2][3] * gradient[2][3]
                )
                change = (
                    sigma_inv * ((viscosity + positive) * laplace[3] + grad_coef * squares)
                    - convect
                    + prod_coef * rate * working
                    - wall_coef * working * jnp.abs(working) / (length * length)
                )
                nu_ref[i, 8 * jb : 8 * jb + 8, :] = working + scale * change

    lax.fori_loop(0, cx, advance, 0)

    for copy in peer_copies + point_copies:
        copy.wait_send()
    for axis in range(3):
        for side in range(2):
            @pl.when(exists(axis, side))
            def _():
                halo_copy(axis, side).wait_send()

    def finish(i, carry):
        for copy in plane_copies(i):
            copy.wait()
        return carry

    lax.fori_loop(0, cx, finish, 0)
    wall_copy.wait()


def hand_over(vel, nu, wall, new_vel, new_nu, wall_out, held, come, go):
    pieces = [(vel.at[f], new_vel.at[f]) for f in range(3)] + [(nu, new_nu), (wall, wall_out)]
    ins = [pltpu.make_async_copy(x, held.at[i], come.at[i]) for i, (x, _) in enumerate(pieces)]
    outs = [pltpu.make_async_copy(held.at[i], y, go.at[i]) for i, (_, y) in enumerate(pieces)]
    for copy in ins:
        copy.start()
    for first, second in zip(ins, outs):
        first.wait()
        second.start()
    for copy in outs:
        copy.wait()


def on_device(
    velocity,
    nu_tilde,
    fluid_cells,
    surface,
    pitch_angle,
    near_tiles,
    send_rows,
    ghost_cell,
    ghost_src,
    ghost_weight,
):
    nx, ny, nz = (lax.axis_size(name) for name in ("gx", "gy", "gz"))
    peers = nx * nz
    _, cx, cy, cz = velocity.shape
    ghosts = ghost_cell.shape[-1]
    points_dev = surface.shape[-1]
    slots = near_tiles.shape[-1]
    hbm = pl.BlockSpec(memory_space=pltpu.HBM)
    f32, i32 = jnp.float32, jnp.int32
    limit = 60 * 1024 * 1024
    results = (
        jax.ShapeDtypeStruct(velocity.shape, f32),
        jax.ShapeDtypeStruct(nu_tilde.shape, f32),
        jax.ShapeDtypeStruct(nu_tilde.shape, f32),
    )
    work = pl.pallas_call(
        functools.partial(step_kernel, (nx, ny, nz)),
        out_shape=results,
        in_specs=[hbm] * 10,
        out_specs=(hbm,) * 3,
        scratch_shapes=[
            pltpu.VMEM((4, cx + 4, cy + 16, cz), f32),
            pltpu.VMEM((4, cx, cy, cz), f32),
            pltpu.VMEM((cx, cy, cz), f32),
            pltpu.VMEM((cx, cy, cz), i32),
            pltpu.VMEM(velocity.shape, f32),
            pltpu.VMEM(nu_tilde.shape, f32),
            pltpu.VMEM((4, cx, cy, cz), f32),
            pltpu.VMEM((3, 1, points_dev), f32),
            pltpu.SMEM((1,), f32),
            pltpu.VMEM((1, slots), i32),
            pltpu.VMEM((peers, LANES), i32),
            pltpu.VMEM((1, ghosts), i32),
            pltpu.VMEM((8, ghosts), i32),
            pltpu.VMEM((8, ghosts), f32),
            pltpu.VMEM((peers, 4, LANES), f32),
            pltpu.VMEM((peers, 4, LANES), f32),
            pltpu.VMEM((ny, 8, points_dev), f32),
            pltpu.VMEM((cx, cy, LANES), f32),
            pltpu.VMEM((4 * LANES, 2 * ghosts), jnp.bfloat16),
            pltpu.VMEM((2 * cx * cy, peers * LANES), jnp.bfloat16),
            pltpu.VMEM((4 * LANES, 2 * cx * cy), jnp.bfloat16),
            pltpu.VMEM((4 * cx * cy // LANES, LANES, LANES), f32),
            pltpu.VMEM((cx * cy, 2 * ghosts), jnp.bfloat16),
            pltpu.VMEM((LANES, ghosts), jnp.bfloat16),
            pltpu.VMEM((2, 8 * cx, cz), f32),
            pltpu.VMEM((2, 8 * cx, cz), f32),
            pltpu.VMEM((2, 8 * cx * cy // LANES, LANES), f32),
            pltpu.VMEM((2, 8 * cx * cy // LANES, LANES), f32),
            pltpu.VMEM((ny * points_dev, cz), f32),
            pltpu.VMEM((ny * points_dev, cz), f32),
            pltpu.VMEM((ny * points_dev, cz), f32),
            pltpu.VMEM((slots, TY, cz), f32),
            pltpu.VMEM((slots, TY, cz), i32),
            pltpu.SemaphoreType.DMA((cx,)),
            pltpu.SemaphoreType.DMA((cx,)),
            pltpu.SemaphoreType.DMA,
            pltpu.SemaphoreType.DMA((10,)),
            pltpu.SemaphoreType.DMA((peers,)),
            pltpu.SemaphoreType.DMA((peers,)),
            pltpu.SemaphoreType.DMA((ny,)),
            pltpu.SemaphoreType.DMA((ny,)),
            pltpu.SemaphoreType.DMA((6,)),
            pltpu.SemaphoreType.DMA((6,)),
        ],
        compiler_params=pltpu.CompilerParams(
            collective_id=0, has_side_effects=True, vmem_limit_bytes=limit
        ),
    )(
        velocity,
        nu_tilde,
        fluid_cells,
        jnp.transpose(surface, (0, 2, 1, 3))[0],
        pitch_angle,
        near_tiles[0, 0],
        send_rows[0, 0, 0],
        ghost_cell[0, 0],
        ghost_src[0, 0, 0],
        ghost_weight[0, 0, 0],
    )
    return pl.pallas_call(
        hand_over,
        out_shape=results,
        in_specs=[hbm] * 3,
        out_specs=(hbm,) * 3,
        scratch_shapes=[
            pltpu.VMEM((5, cx, cy, cz), f32),
            pltpu.SemaphoreType.DMA((5,)),
            pltpu.SemaphoreType.DMA((5,)),
        ],
        compiler_params=pltpu.CompilerParams(vmem_limit_bytes=limit),
    )(*work)


def solution(mesh):
    in_specs = (
        P(None, "gx", "gy", "gz"),
        P("gx", "gy", "gz"),
        P("gx", "gy", "gz"),
        P("gx", "gz", None, "gy"),
        P(),
        P("gx", "gy", "gz", None),
        P("gx", "gy", "gz", None, None),
        P("gx", "gy", "gz", None),
        P("gx", "gy", "gz", None, None),
        P("gx", "gy", "gz", None, None),
    )
    out_specs = (P(None, "gx", "gy", "gz"), P("gx", "gy", "gz"), P("gx", "gy", "gz"))
    return jax.shard_map(
        on_device, mesh=mesh, in_specs=in_specs, out_specs=out_specs, check_vma=False
    )
```

```python
import functools

import jax
import jax.numpy as jnp
from jax import lax
from jax.experimental import pallas as pl
from jax.experimental.pallas import tpu as pltpu
from jax.sharding import PartitionSpec as P

MESH = pl.DeviceIdType.MESH
TY = 8
LANES = 128

viscosity = 0.2
prod_coef = 0.1355
grad_coef = 0.622
sigma_inv = 1.5
karman = 0.41
visc_coef = 7.1
wall_coef = prod_coef / (karman * karman) + (1.0 + grad_coef) * sigma_inv
des_coef = 0.65
floor_rate = 0.3
dist_eps = 0.25
dist_cap = 8.0
time_step = 0.05


def lookup(row, lanes):
    table = jnp.broadcast_to(row, lanes.shape)
    return lax.gather(
        table,
        lanes[:, :, None],
        lax.GatherDimensionNumbers(
            offset_dims=(),
            collapsed_slice_dims=(1,),
            start_index_map=(1,),
            operand_batching_dims=(0,),
            start_indices_batching_dims=(0,),
        ),
        slice_sizes=(1, 1),
        mode=lax.GatherScatterMode.PROMISE_IN_BOUNDS,
    )


def fill_kernel(
    sizes,
    vel_hbm,
    nu_hbm,
    surf_hbm,
    pitch_hbm,
    tiles_hbm,
    rows_hbm,
    cell_hbm,
    src_hbm,
    weight_hbm,
    core,
    halo_x,
    halo_y,
    halo_z,
    wall_out,
    filled,
    wall_ref,
    fields,
    surf_ref,
    pitch_ref,
    tiles_ref,
    rows_ref,
    cell_ref,
    src_ref,
    weight_ref,
    out_buf,
    in_buf,
    points,
    is_ghost,
    spread,
    choose,
    parts,
    by_row,
    by_lane,
    pack_y,
    pack_z,
    flat_x,
    flat_y,
    flat_z2,
    dist,
    tile_of,
    core_sem,
    wall_sem,
    load,
    peer_send,
    peer_recv,
    point_send,
    point_recv,
    halo_send,
    halo_recv,
):
    pairs = (
        (pitch_hbm, pitch_ref),
        (surf_hbm, surf_ref),
        (rows_hbm, rows_ref),
        (vel_hbm, fields.at[0:3]),
        (nu_hbm, fields.at[3]),
        (cell_hbm, cell_ref),
        (src_hbm, src_ref),
        (weight_hbm, weight_ref),
        (tiles_hbm, tiles_ref),
    )
    loads = [pltpu.make_async_copy(x, y, load.at[i]) for i, (x, y) in enumerate(pairs)]
    for copy in loads:
        copy.start()

    nx, ny, nz = sizes
    peers = nx * nz
    _, cx, cy, cz = vel_hbm.shape
    rows_y = cy // 8
    chunks = cell_hbm.shape[1] // LANES
    a, b, c = (lax.axis_index(name) for name in ("gx", "gy", "gz"))
    me = a * nz + c
    lane = lax.broadcasted_iota(jnp.int32, (8, LANES), 1)
    slots = tiles_hbm.shape[1]
    per_row = cy // TY

    def peer_of(d):
        other = lax.rem(me + d, peers)
        return other, (lax.div(other, nz), b, lax.rem(other, nz))

    def column_of(d):
        other = lax.rem(b + d, ny)
        return other, (a, other, c)

    barrier = pltpu.get_barrier_semaphore()
    for d in range(1, peers):
        pl.semaphore_signal(barrier, inc=1, device_id=peer_of(d)[1], device_id_type=MESH)
    for d in range(1, ny):
        pl.semaphore_signal(barrier, inc=1, device_id=column_of(d)[1], device_id_type=MESH)

    for copy in loads[0:2]:
        copy.wait()
    angle = jnp.full((1, LANES), pitch_ref[0], jnp.float32)
    cosine, sine = jnp.cos(angle), jnp.sin(angle)
    px, py, pz = surf_ref[0], surf_ref[1], surf_ref[2]
    points[b] = jnp.concatenate(
        [cosine * px + sine * pz, py, cosine * pz - sine * px, jnp.zeros((5, LANES), jnp.float32)], axis=0
    )

    pl.semaphore_wait(barrier, peers - 1 + ny - 1)

    def point_copy(d):
        return pltpu.make_async_remote_copy(
            src_ref=points.at[b],
            dst_ref=points.at[b],
            send_sem=point_send.at[d],
            recv_sem=point_recv.at[d],
            device_id=column_of(d)[1],
            device_id_type=MESH,
        )

    point_copies = [point_copy(d) for d in range(1, ny)]
    for copy in point_copies:
        copy.start()

    cells_hi = cx * cy
    loads[2].wait()
    row_number = lax.broadcasted_iota(jnp.int32, (cells_hi, LANES), 0)
    lane_number = lax.broadcasted_iota(jnp.int32, (LANES, 2 * LANES), 0)
    for p in range(peers):
        wanted = lax.shift_right_arithmetic(rows_ref[p : p + 1, :], 7)
        hit = jnp.where(row_number == wanted, 1.0, 0.0).astype(jnp.bfloat16)
        choose[0:cells_hi, LANES * p : LANES * (p + 1)] = hit
        choose[cells_hi : 2 * cells_hi, LANES * p : LANES * (p + 1)] = hit

    for copy in loads[3:5]:
        copy.wait()
    for f in range(4):
        across = fields[f].reshape(cells_hi, LANES).T
        big = across.astype(jnp.bfloat16)
        rest = (across - big.astype(jnp.float32)).astype(jnp.bfloat16)
        parts[LANES * f : LANES * (f + 1), 0:cells_hi] = big
        parts[LANES * f : LANES * (f + 1), cells_hi : 2 * cells_hi] = rest

    def pick(k, carry):
        at = pl.multiple_of(k * 2 * LANES, 2 * LANES)
        found = jnp.dot(
            parts[...], choose[:, pl.ds(at, 2 * LANES)], preferred_element_type=jnp.float32
        )
        both = jnp.concatenate([rows_ref[pl.ds(2 * k, 1), :], rows_ref[pl.ds(2 * k + 1, 1), :]], axis=1)
        here = lane_number == (both & (LANES - 1))
        for f in range(4):
            row = jnp.sum(
                jnp.where(here, found[LANES * f : LANES * (f + 1), :], 0.0), axis=0, keepdims=True
            )
            out_buf[2 * k, f : f + 1, :] = row[:, 0:LANES]
            out_buf[2 * k + 1, f : f + 1, :] = row[:, LANES : 2 * LANES]
        return carry

    lax.fori_loop(0, peers // 2, pick, 0, unroll=peers <= 8)

    def peer_copy(d):
        other, device = peer_of(d)
        return pltpu.make_async_remote_copy(
            src_ref=out_buf.at[other],
            dst_ref=in_buf.at[me],
            send_sem=peer_send.at[d],
            recv_sem=peer_recv.at[d],
            device_id=device,
            device_id_type=MESH,
        )

    peer_copies = [peer_copy(d) for d in range(1, peers)]
    for copy in peer_copies:
        copy.start()
    in_buf[me] = out_buf[me]

    for copy in loads[5:]:
        copy.wait()

    for copy in point_copies:
        copy.wait_recv()
    deep = (lax.broadcasted_iota(jnp.int32, (LANES, LANES), 1).astype(jnp.float32) + 0.5) - 0.5 * cz
    for g in range(ny):
        at = slice(LANES * g, LANES * (g + 1))
        flat_x[at, :] = jnp.broadcast_to(points[g, 0:1, :], (LANES, LANES)).T
        flat_y[at, :] = jnp.broadcast_to(points[g, 1:2, :], (LANES, LANES)).T
        step_z = deep - jnp.broadcast_to(points[g, 2:3, :], (LANES, LANES)).T
        flat_z2[at, :] = step_z * step_z

    for s in range(slots):
        tile_of[s] = jnp.broadcast_to(tiles_ref[0:1, s : s + 1], (8, LANES))

    def one_slot(s, carry):
        tile = jnp.maximum(tile_of[s], 0)
        at_x = lax.div(tile, per_row).astype(jnp.float32) + (0.5 - 0.5 * cx)
        first = lax.rem(tile, per_row) * TY + b * cy
        at_y = first.astype(jnp.float32) + (0.5 - 0.5 * (ny * cy))

        def some_points(k, best):
            for u in range(16):
                at = pl.ds(pl.multiple_of(k * LANES, LANES) + 8 * u, 8)
                step_x = at_x - flat_x[at, :]
                step_y = at_y - flat_y[at, :]
                value = (step_x * step_x + step_y * step_y) + flat_z2[at, :]
                twice = step_y + step_y
                new = [jnp.minimum(best[0], value)]
                for r in range(1, TY):
                    value = value + twice
                    new.append(jnp.minimum(best[r], value))
                best = tuple(new)
            return best

        start = tuple(jnp.full((8, LANES), jnp.inf, jnp.float32) for _ in range(TY))
        best = lax.fori_loop(0, ny, some_points, start)
        least = jnp.concatenate(
            [jnp.min(x, axis=0, keepdims=True) + float(r * r) for r, x in enumerate(best)], axis=0
        )
        dist[s] = jnp.minimum(jnp.sqrt(least + dist_eps), dist_cap)
        return carry

    ghosts = cell_ref.shape[1]
    cells = cell_ref[...]
    row_id = lax.broadcasted_iota(jnp.int32, (cells_hi, ghosts), 0)
    lane_id = lax.broadcasted_iota(jnp.int32, (LANES, ghosts), 0)
    hit_row = jnp.where(row_id == lax.shift_right_arithmetic(cells, 7), 1.0, 0.0).astype(jnp.bfloat16)
    by_row[:, 0:ghosts] = hit_row
    by_row[:, ghosts : 2 * ghosts] = hit_row
    by_lane[...] = jnp.where(lane_id == (cells & (LANES - 1)), 1.0, 0.0).astype(jnp.bfloat16)
    last_dims = (((1,), (1,)), ((), ()))
    is_ghost[...] = lax.dot_general(
        by_row[:, 0:ghosts], by_lane[...], last_dims, preferred_element_type=jnp.float32
    ).reshape(cx, cy, LANES)

    lax.fori_loop(0, slots // 2, one_slot, 0)

    for copy in peer_copies:
        copy.wait_recv()

    def interpolate(m, carry):
        at = pl.ds(pl.multiple_of(m * LANES, LANES), LANES)
        source = src_ref[:, at]
        weight = weight_ref[:, at]
        from_peer = lax.shift_right_arithmetic(source, 7)
        from_slot = source & (LANES - 1)

        def one_peer(p, acc):
            here = from_peer == p
            return tuple(
                jnp.where(here, lookup(in_buf[p, f : f + 1, :], from_slot), acc[f]) for f in range(4)
            )

        acc = tuple(jnp.zeros((8, LANES), jnp.float32) for _ in range(4))
        if peers <= 8:
            for p in range(peers):
                acc = one_peer(p, acc)
        else:
            acc = lax.fori_loop(0, peers, one_peer, acc)
        for f in range(4):
            value = -jnp.sum(weight * acc[f], axis=0, keepdims=True)
            big = value.astype(jnp.bfloat16)
            rest = (value - big.astype(jnp.float32)).astype(jnp.bfloat16)
            hit = by_lane[:, at]
            to = pl.ds(pl.multiple_of(ghosts + m * LANES, LANES), LANES)
            spread[LANES * f : LANES * (f + 1), at] = hit * jnp.broadcast_to(big, hit.shape)
            spread[LANES * f : LANES * (f + 1), to] = hit * jnp.broadcast_to(rest, hit.shape)
        return carry

    lax.fori_loop(0, chunks, interpolate, 0, unroll=4 if peers <= 8 else 1)

    stored = lax.dot_general(by_row[...], spread[...], last_dims, preferred_element_type=jnp.float32)
    for f in range(4):
        value = stored[:, LANES * f : LANES * (f + 1)].reshape(cx, cy, LANES)
        filled[f] = jnp.where(is_ghost[...] > 0.5, value, fields[f])

    low_high = ((a, nx), (b, ny), (c, nz))

    def exists(axis, side):
        index, count = low_high[axis]
        return index > 0 if side == 0 else index < count - 1

    def beside(axis, side):
        place = [a, b, c]
        place[axis] = place[axis] + (1 if side else -1)
        return tuple(place)

    def halo_copy(axis, side, arrives):
        if axis == 0:
            source = filled.at[:, 0:2] if side == 0 else filled.at[:, cx - 2 : cx]
        else:
            source = (pack_y, pack_z)[axis - 1].at[side]
        end = side if arrives else 1 - side
        return pltpu.make_async_remote_copy(
            src_ref=source,
            dst_ref=(halo_x, halo_y, halo_z)[axis].at[end],
            send_sem=halo_send.at[2 * axis + side],
            recv_sem=halo_recv.at[2 * axis + end],
            device_id=beside(axis, side),
            device_id_type=MESH,
        )

    def send_halo(axis):
        for side in range(2):
            @pl.when(exists(axis, side))
            def _():
                halo_copy(axis, side, False).start()

    def wait_halo(axis):
        for side in range(2):
            @pl.when(exists(axis, side))
            def _():
                halo_copy(axis, side, True).wait_recv()

    send_halo(0)
    core_copy = pltpu.make_async_copy(filled, core, core_sem)
    core_copy.start()
    for f in range(4):
        for i in range(cx):
            at = 2 * (f * cx + i)
            pack_y[0, at : at + 2, :] = filled[f, i, 0:2, :]
            pack_y[1, at : at + 2, :] = filled[f, i, cy - 2 : cy, :]
    send_halo(1)
    planes = LANES // cy
    blocks = cx // planes
    for f in range(4):
        for g in range(blocks):
            block = filled[f, planes * g : planes * (g + 1)].reshape(LANES, LANES)
            across = block.T
            at = 2 * (f * blocks + g)
            pack_z[0, at : at + 2, :] = across[0:2, :]
            pack_z[1, at : at + 2, :] = across[LANES - 2 : LANES, :]
    send_halo(2)

    lax.fori_loop(slots // 2, slots, one_slot, 0)

    def place(i, carry):
        for jb in range(rows_y):
            wall = jnp.full((8, LANES), dist_cap, jnp.float32)
            for s in range(slots):
                wall = jnp.where(tile_of[s] == i * per_row + jb, dist[s], wall)
            wall_ref[i, 8 * jb : 8 * jb + 8, :] = wall
        return carry

    lax.fori_loop(0, cx, place, 0)
    wall_copy = pltpu.make_async_copy(wall_ref, wall_out, wall_sem)
    wall_copy.start()

    for axis in range(3):
        wait_halo(axis)
    for copy in peer_copies + point_copies:
        copy.wait_send()
    for axis in range(3):
        for side in range(2):
            @pl.when(exists(axis, side))
            def _():
                halo_copy(axis, side, False).wait_send()

    core_copy.wait()
    wall_copy.wait()


def step_kernel(
    sizes,
    core,
    halo_x,
    halo_y,
    halo_z,
    wall_hbm,
    fluid_hbm,
    new_vel,
    new_nu,
    wall_out,
    padded,
    got_y,
    got_z,
    wall_ref,
    fluid_ref,
    turn,
    edge_z,
    vel_ref,
    nu_ref,
    load,
    halo_load,
    wall_sem,
    vel_sem,
    nu_sem,
):
    cx, cy, _ = wall_ref.shape
    rows_y = cy // 8
    planes = LANES // cy
    blocks = cx // planes
    lane = lax.broadcasted_iota(jnp.int32, (8, LANES), 1)
    place = [lax.axis_index(name) for name in ("gx", "gy", "gz")]
    margin_x = (padded.at[:, 0:2, 8 : 8 + cy, :], padded.at[:, cx + 2 : cx + 4, 8 : 8 + cy, :])
    targets = (margin_x, (got_y.at[0], got_y.at[1]), (got_z.at[0], got_z.at[1]))

    def exists(axis, side):
        return place[axis] > 0 if side == 0 else place[axis] < sizes[axis] - 1

    def halo_copy(axis, side):
        source = (halo_x, halo_y, halo_z)[axis].at[side]
        return pltpu.make_async_copy(source, targets[axis][side], halo_load.at[2 * axis + side])

    core_copy = pltpu.make_async_copy(core, padded.at[:, 2 : cx + 2, 8 : 8 + cy, :], load.at[0])
    wall_copy = pltpu.make_async_copy(wall_hbm, wall_ref, load.at[1])
    fluid_copy = pltpu.make_async_copy(fluid_hbm, fluid_ref, load.at[2])
    for axis in (2, 1, 0):
        for side in range(2):
            @pl.when(exists(axis, side))
            def _():
                halo_copy(axis, side).start()

    core_copy.start()
    wall_copy.start()
    fluid_copy.start()
    for axis in (2, 1, 0):
        for side in range(2):
            target = targets[axis][side]

            @pl.when(jnp.logical_not(exists(axis, side)))
            def _():
                target[...] = jnp.zeros(target.shape, jnp.float32)

    for axis in (2, 1, 0):
        for side in range(2):
            @pl.when(exists(axis, side))
            def _():
                halo_copy(axis, side).wait()

    for f in range(4):
        for g in range(blocks):
            at = 2 * (f * blocks + g)
            turn[f * blocks + g, 0:2, :] = got_z[1, at : at + 2, :]
            turn[f * blocks + g, LANES - 2 : LANES, :] = got_z[0, at : at + 2, :]
            edge_z[f, planes * g : planes * (g + 1), :, :] = turn[f * blocks + g].T.reshape(planes, cy, LANES)
    for f in range(4):
        for i in range(cx):
            at = 2 * (f * cx + i)
            padded[f, i + 2, 6:8, :] = got_y[0, at : at + 2, :]
            padded[f, i + 2, 8 + cy : 10 + cy, :] = got_y[1, at : at + 2, :]

    core_copy.wait()
    wall_copy.wait()
    fluid_copy.wait()
    show_wall = pltpu.make_async_copy(wall_ref, wall_out, wall_sem)
    show_wall.start()

    def plane_copies(i):
        return (
            pltpu.make_async_copy(vel_ref.at[:, i], new_vel.at[:, i], vel_sem.at[i]),
            pltpu.make_async_copy(nu_ref.at[i], new_nu.at[i], nu_sem.at[i]),
        )

    def advance(i, carry):
        for jb in range(rows_y):
            advance_rows(i, jb)
        for copy in plane_copies(i):
            copy.start()
        return carry

    def advance_rows(i, jb):
        center, gradient, laplace = [], [[], [], []], []

        def slope(m2, m1, p1, p2):
            return ((m2 - p2) + 8.0 * (p1 - m1)) * (1.0 / 12.0)

        for f in range(4):
            begin = 8 + 8 * jb
            mid = padded[f, i + 2, begin : begin + 8, :]
            x = [padded[f, i + 2 + h, begin : begin + 8, :] for h in (-2, -1, 1, 2)]
            y = [padded[f, i + 2, begin + h : begin + h + 8, :] for h in (-2, -1, 1, 2)]
            rim = edge_z[f, i, 8 * jb : 8 * jb + 8, :]
            z = [
                pltpu.roll(jnp.where(lane >= LANES - 2, rim, mid), 2, 1),
                pltpu.roll(jnp.where(lane >= LANES - 1, rim, mid), 1, 1),
                pltpu.roll(jnp.where(lane < 1, rim, mid), LANES - 1, 1),
                pltpu.roll(jnp.where(lane < 2, rim, mid), LANES - 2, 1),
            ]
            center.append(mid)
            for e, line in enumerate((x, y, z)):
                gradient[e].append(slope(*line))
            laplace.append(((x[1] + x[2]) + (y[1] + y[2])) + ((z[1] + z[2]) - 6.0 * mid))
        u, v, w, working = center
        curl_x = gradient[1][2] - gradient[2][1]
        curl_y = gradient[2][0] - gradient[0][2]
        curl_z = gradient[0][1] - gradient[1][0]
        rate = jnp.maximum(jnp.sqrt(curl_x * curl_x + curl_y * curl_y + curl_z * curl_z), floor_rate)
        positive = jnp.maximum(working, 0.0)
        chi = positive * (1.0 / viscosity)
        chi_cubed = chi * chi * chi
        diffusion = viscosity + positive * chi_cubed / (chi_cubed + visc_coef**3)
        wall = wall_ref[i, 8 * jb : 8 * jb + 8, :]
        arg = (8.0 * diffusion) / (rate * (karman * karman) * (wall * wall))
        shield = 1.0 - jnp.tanh(arg * arg * arg)
        length = wall - shield * jnp.maximum(wall - des_coef, 0.0)
        scale = time_step * fluid_ref[i, 8 * jb : 8 * jb + 8, :].astype(jnp.float32)
        for f in range(4):
            convect = u * gradient[0][f] + v * gradient[1][f] + w * gradient[2][f]
            if f < 3:
                change = diffusion * laplace[f] - convect
                vel_ref[f, i, 8 * jb : 8 * jb + 8, :] = center[f] + scale * change
            else:
                squares = (
                    gradient[0][3] * gradient[0][3]
                    + gradient[1][3] * gradient[1][3]
                    + gradient[2][3] * gradient[2][3]
                )
                change = (
                    sigma_inv * ((viscosity + positive) * laplace[3] + grad_coef * squares)
                    - convect
                    + prod_coef * rate * working
                    - wall_coef * working * jnp.abs(working) / (length * length)
                )
                nu_ref[i, 8 * jb : 8 * jb + 8, :] = working + scale * change

    lax.fori_loop(0, cx, advance, 0)

    def finish(i, carry):
        for copy in plane_copies(i):
            copy.wait()
        return carry

    lax.fori_loop(0, cx, finish, 0)
    show_wall.wait()


def on_device(
    velocity,
    nu_tilde,
    fluid_cells,
    surface,
    pitch_angle,
    near_tiles,
    send_rows,
    ghost_cell,
    ghost_src,
    ghost_weight,
):
    nx, ny, nz = (lax.axis_size(name) for name in ("gx", "gy", "gz"))
    peers = nx * nz
    _, cx, cy, cz = velocity.shape
    ghosts = ghost_cell.shape[-1]
    points_dev = surface.shape[-1]
    slots = near_tiles.shape[-1]
    hbm = pl.BlockSpec(memory_space=pltpu.HBM)
    f32, i32 = jnp.float32, jnp.int32
    limit = 60 * 1024 * 1024
    edge = 8 * cx * cy // LANES
    work = pl.pallas_call(
        functools.partial(fill_kernel, (nx, ny, nz)),
        out_shape=(
            jax.ShapeDtypeStruct((4, cx, cy, cz), f32),
            jax.ShapeDtypeStruct((2, 4, 2, cy, cz), f32),
            jax.ShapeDtypeStruct((2, 8 * cx, cz), f32),
            jax.ShapeDtypeStruct((2, edge, LANES), f32),
            jax.ShapeDtypeStruct((cx, cy, cz), f32),
        ),
        in_specs=[hbm] * 9,
        out_specs=(hbm,) * 5,
        scratch_shapes=[
            pltpu.VMEM((4, cx, cy, cz), f32),
            pltpu.VMEM((cx, cy, cz), f32),
            pltpu.VMEM((4, cx, cy, cz), f32),
            pltpu.VMEM((3, 1, points_dev), f32),
            pltpu.SMEM((1,), f32),
            pltpu.VMEM((1, slots), i32),
            pltpu.VMEM((peers, LANES), i32),
            pltpu.VMEM((1, ghosts), i32),
            pltpu.VMEM((8, ghosts), i32),
            pltpu.VMEM((8, ghosts), f32),
            pltpu.VMEM((peers, 4, LANES), f32),
            pltpu.VMEM((peers, 4, LANES), f32),
            pltpu.VMEM((ny, 8, points_dev), f32),
            pltpu.VMEM((cx, cy, LANES), f32),
            pltpu.VMEM((4 * LANES, 2 * ghosts), jnp.bfloat16),
            pltpu.VMEM((2 * cx * cy, peers * LANES), jnp.bfloat16),
            pltpu.VMEM((4 * LANES, 2 * cx * cy), jnp.bfloat16),
            pltpu.VMEM((cx * cy, 2 * ghosts), jnp.bfloat16),
            pltpu.VMEM((LANES, ghosts), jnp.bfloat16),
            pltpu.VMEM((2, 8 * cx, cz), f32),
            pltpu.VMEM((2, edge, LANES), f32),
            pltpu.VMEM((ny * points_dev, cz), f32),
            pltpu.VMEM((ny * points_dev, cz), f32),
            pltpu.VMEM((ny * points_dev, cz), f32),
            pltpu.VMEM((slots, TY, cz), f32),
            pltpu.VMEM((slots, TY, cz), i32),
            pltpu.SemaphoreType.DMA,
            pltpu.SemaphoreType.DMA,
            pltpu.SemaphoreType.DMA((9,)),
            pltpu.SemaphoreType.DMA((peers,)),
            pltpu.SemaphoreType.DMA((peers,)),
            pltpu.SemaphoreType.DMA((ny,)),
            pltpu.SemaphoreType.DMA((ny,)),
            pltpu.SemaphoreType.DMA((6,)),
            pltpu.SemaphoreType.DMA((6,)),
        ],
        compiler_params=pltpu.CompilerParams(
            collective_id=0, has_side_effects=True, vmem_limit_bytes=limit
        ),
    )(
        velocity,
        nu_tilde,
        jnp.transpose(surface, (0, 2, 1, 3))[0],
        pitch_angle,
        near_tiles[0, 0],
        send_rows[0, 0, 0],
        ghost_cell[0, 0],
        ghost_src[0, 0, 0],
        ghost_weight[0, 0, 0],
    )
    return pl.pallas_call(
        functools.partial(step_kernel, (nx, ny, nz)),
        out_shape=(
            jax.ShapeDtypeStruct(velocity.shape, f32),
            jax.ShapeDtypeStruct(nu_tilde.shape, f32),
            jax.ShapeDtypeStruct(nu_tilde.shape, f32),
        ),
        in_specs=[hbm] * 6,
        out_specs=(hbm,) * 3,
        scratch_shapes=[
            pltpu.VMEM((4, cx + 4, cy + 16, cz), f32),
            pltpu.VMEM((2, 8 * cx, cz), f32),
            pltpu.VMEM((2, edge, LANES), f32),
            pltpu.VMEM((cx, cy, cz), f32),
            pltpu.VMEM((cx, cy, cz), i32),
            pltpu.VMEM((4 * cx * cy // LANES, LANES, LANES), f32),
            pltpu.VMEM((4, cx, cy, cz), f32),
            pltpu.VMEM(velocity.shape, f32),
            pltpu.VMEM(nu_tilde.shape, f32),
            pltpu.SemaphoreType.DMA((3,)),
            pltpu.SemaphoreType.DMA((6,)),
            pltpu.SemaphoreType.DMA,
            pltpu.SemaphoreType.DMA((cx,)),
            pltpu.SemaphoreType.DMA((cx,)),
        ],
        compiler_params=pltpu.CompilerParams(vmem_limit_bytes=limit),
    )(*work, fluid_cells)


def solution(mesh):
    in_specs = (
        P(None, "gx", "gy", "gz"),
        P("gx", "gy", "gz"),
        P("gx", "gy", "gz"),
        P("gx", "gz", None, "gy"),
        P(),
        P("gx", "gy", "gz", None),
        P("gx", "gy", "gz", None, None),
        P("gx", "gy", "gz", None),
        P("gx", "gy", "gz", None, None),
        P("gx", "gy", "gz", None, None),
    )
    out_specs = (P(None, "gx", "gy", "gz"), P("gx", "gy", "gz"), P("gx", "gy", "gz"))
    return jax.shard_map(
        on_device, mesh=mesh, in_specs=in_specs, out_specs=out_specs, check_vma=False
    )
```

```python
import functools

import jax
import jax.numpy as jnp
from jax import lax
from jax.experimental import pallas as pl
from jax.experimental.pallas import tpu as pltpu
from jax.sharding import PartitionSpec as P

MESH = pl.DeviceIdType.MESH
TY = 8
LANES = 128

viscosity = 0.2
prod_coef = 0.1355
grad_coef = 0.622
sigma_inv = 1.5
karman = 0.41
visc_coef = 7.1
wall_coef = prod_coef / (karman * karman) + (1.0 + grad_coef) * sigma_inv
des_coef = 0.65
floor_rate = 0.3
dist_eps = 0.25
dist_cap = 8.0
time_step = 0.05


def lookup(row, lanes):
    table = jnp.broadcast_to(row, lanes.shape)
    return lax.gather(
        table,
        lanes[:, :, None],
        lax.GatherDimensionNumbers(
            offset_dims=(),
            collapsed_slice_dims=(1,),
            start_index_map=(1,),
            operand_batching_dims=(0,),
            start_indices_batching_dims=(0,),
        ),
        slice_sizes=(1, 1),
        mode=lax.GatherScatterMode.PROMISE_IN_BOUNDS,
    )


def fill_kernel(
    sizes,
    vel_hbm,
    nu_hbm,
    surf_hbm,
    pitch_hbm,
    tiles_hbm,
    rows_hbm,
    cell_hbm,
    src_hbm,
    weight_hbm,
    core,
    halo_x,
    halo_y,
    halo_z,
    wall_out,
    filled,
    wall_ref,
    fields,
    surf_ref,
    pitch_ref,
    tiles_ref,
    rows_ref,
    cell_ref,
    src_ref,
    weight_ref,
    out_buf,
    in_buf,
    points,
    is_ghost,
    spread,
    choose,
    parts,
    by_row,
    by_lane,
    pack_y,
    pack_z,
    flat_x,
    flat_y,
    flat_z2,
    dist,
    tile_of,
    core_sem,
    wall_sem,
    load,
    peer_send,
    peer_recv,
    point_send,
    point_recv,
    halo_send,
    halo_recv,
):
    pairs = (
        (pitch_hbm, pitch_ref),
        (surf_hbm, surf_ref),
        (rows_hbm, rows_ref),
        (vel_hbm, fields.at[0:3]),
        (nu_hbm, fields.at[3]),
        (cell_hbm, cell_ref),
        (src_hbm, src_ref),
        (weight_hbm, weight_ref),
        (tiles_hbm, tiles_ref),
    )
    loads = [pltpu.make_async_copy(x, y, load.at[i]) for i, (x, y) in enumerate(pairs)]
    for copy in loads:
        copy.start()

    nx, ny, nz = sizes
    peers = nx * nz
    _, cx, cy, cz = vel_hbm.shape
    rows_y = cy // 8
    chunks = cell_hbm.shape[1] // LANES
    a, b, c = (lax.axis_index(name) for name in ("gx", "gy", "gz"))
    me = a * nz + c
    lane = lax.broadcasted_iota(jnp.int32, (8, LANES), 1)
    slots = tiles_hbm.shape[1]
    per_row = cy // TY

    def peer_of(d):
        other = lax.rem(me + d, peers)
        return other, (lax.div(other, nz), b, lax.rem(other, nz))

    def column_of(d):
        other = lax.rem(b + d, ny)
        return other, (a, other, c)

    barrier = pltpu.get_barrier_semaphore()
    for d in range(1, peers):
        pl.semaphore_signal(barrier, inc=1, device_id=peer_of(d)[1], device_id_type=MESH)
    for d in range(1, ny):
        pl.semaphore_signal(barrier, inc=1, device_id=column_of(d)[1], device_id_type=MESH)

    for copy in loads[0:2]:
        copy.wait()
    angle = jnp.full((1, LANES), pitch_ref[0], jnp.float32)
    cosine, sine = jnp.cos(angle), jnp.sin(angle)
    px, py, pz = surf_ref[0], surf_ref[1], surf_ref[2]
    points[b] = jnp.concatenate(
        [cosine * px + sine * pz, py, cosine * pz - sine * px, jnp.zeros((5, LANES), jnp.float32)], axis=0
    )

    pl.semaphore_wait(barrier, peers - 1 + ny - 1)

    def point_copy(d):
        return pltpu.make_async_remote_copy(
            src_ref=points.at[b],
            dst_ref=points.at[b],
            send_sem=point_send.at[d],
            recv_sem=point_recv.at[d],
            device_id=column_of(d)[1],
            device_id_type=MESH,
        )

    point_copies = [point_copy(d) for d in range(1, ny)]
    for copy in point_copies:
        copy.start()

    cells_hi = cx * cy
    loads[2].wait()
    row_number = lax.broadcasted_iota(jnp.int32, (cells_hi, LANES), 0)
    lane_number = lax.broadcasted_iota(jnp.int32, (LANES, 2 * LANES), 0)
    for p in range(peers):
        wanted = lax.shift_right_arithmetic(rows_ref[p : p + 1, :], 7)
        hit = jnp.where(row_number == wanted, 1.0, 0.0).astype(jnp.bfloat16)
        choose[0:cells_hi, LANES * p : LANES * (p + 1)] = hit
        choose[cells_hi : 2 * cells_hi, LANES * p : LANES * (p + 1)] = hit

    for copy in loads[3:5]:
        copy.wait()
    for f in range(4):
        across = fields[f].reshape(cells_hi, LANES).T
        big = across.astype(jnp.bfloat16)
        rest = (across - big.astype(jnp.float32)).astype(jnp.bfloat16)
        parts[LANES * f : LANES * (f + 1), 0:cells_hi] = big
        parts[LANES * f : LANES * (f + 1), cells_hi : 2 * cells_hi] = rest

    def pick(k, carry):
        at = pl.multiple_of(k * 2 * LANES, 2 * LANES)
        found = jnp.dot(
            parts[...], choose[:, pl.ds(at, 2 * LANES)], preferred_element_type=jnp.float32
        )
        both = jnp.concatenate([rows_ref[pl.ds(2 * k, 1), :], rows_ref[pl.ds(2 * k + 1, 1), :]], axis=1)
        here = lane_number == (both & (LANES - 1))
        for f in range(4):
            row = jnp.sum(
                jnp.where(here, found[LANES * f : LANES * (f + 1), :], 0.0), axis=0, keepdims=True
            )
            out_buf[2 * k, f : f + 1, :] = row[:, 0:LANES]
            out_buf[2 * k + 1, f : f + 1, :] = row[:, LANES : 2 * LANES]
        return carry

    lax.fori_loop(0, peers // 2, pick, 0, unroll=peers <= 8)

    def peer_copy(d):
        other, device = peer_of(d)
        return pltpu.make_async_remote_copy(
            src_ref=out_buf.at[other],
            dst_ref=in_buf.at[me],
            send_sem=peer_send.at[d],
            recv_sem=peer_recv.at[d],
            device_id=device,
            device_id_type=MESH,
        )

    peer_copies = [peer_copy(d) for d in range(1, peers)]
    for copy in peer_copies:
        copy.start()
    in_buf[me] = out_buf[me]

    for copy in loads[5:]:
        copy.wait()

    for copy in point_copies:
        copy.wait_recv()
    deep = (lax.broadcasted_iota(jnp.int32, (LANES, LANES), 1).astype(jnp.float32) + 0.5) - 0.5 * cz
    for g in range(ny):
        at = slice(LANES * g, LANES * (g + 1))
        flat_x[at, :] = jnp.broadcast_to(points[g, 0:1, :], (LANES, LANES)).T
        flat_y[at, :] = jnp.broadcast_to(points[g, 1:2, :], (LANES, LANES)).T
        step_z = deep - jnp.broadcast_to(points[g, 2:3, :], (LANES, LANES)).T
        flat_z2[at, :] = step_z * step_z

    for s in range(slots):
        tile_of[s] = jnp.broadcast_to(tiles_ref[0:1, s : s + 1], (8, LANES))

    def one_slot(s, carry):
        tile = jnp.maximum(tile_of[s], 0)
        at_x = lax.div(tile, per_row).astype(jnp.float32) + (0.5 - 0.5 * cx)
        first = lax.rem(tile, per_row) * TY + b * cy
        at_y = first.astype(jnp.float32) + (0.5 - 0.5 * (ny * cy))

        def some_points(k, best):
            for u in range(16):
                at = pl.ds(pl.multiple_of(k * LANES, LANES) + 8 * u, 8)
                step_x = at_x - flat_x[at, :]
                step_y = at_y - flat_y[at, :]
                value = (step_x * step_x + step_y * step_y) + flat_z2[at, :]
                twice = step_y + step_y
                new = [jnp.minimum(best[0], value)]
                for r in range(1, TY):
                    value = value + twice
                    new.append(jnp.minimum(best[r], value))
                best = tuple(new)
            return best

        start = tuple(jnp.full((8, LANES), jnp.inf, jnp.float32) for _ in range(TY))
        best = lax.fori_loop(0, ny, some_points, start)
        least = jnp.concatenate(
            [jnp.min(x, axis=0, keepdims=True) + float(r * r) for r, x in enumerate(best)], axis=0
        )
        dist[s] = jnp.minimum(jnp.sqrt(least + dist_eps), dist_cap)
        return carry

    ghosts = cell_ref.shape[1]
    cells = cell_ref[...]
    row_id = lax.broadcasted_iota(jnp.int32, (cells_hi, ghosts), 0)
    lane_id = lax.broadcasted_iota(jnp.int32, (LANES, ghosts), 0)
    hit_row = jnp.where(row_id == lax.shift_right_arithmetic(cells, 7), 1.0, 0.0).astype(jnp.bfloat16)
    by_row[:, 0:ghosts] = hit_row
    by_row[:, ghosts : 2 * ghosts] = hit_row
    by_lane[...] = jnp.where(lane_id == (cells & (LANES - 1)), 1.0, 0.0).astype(jnp.bfloat16)
    last_dims = (((1,), (1,)), ((), ()))
    is_ghost[...] = lax.dot_general(
        by_row[:, 0:ghosts], by_lane[...], last_dims, preferred_element_type=jnp.float32
    ).reshape(cx, cy, LANES)

    early = slots * 3 // 4
    lax.fori_loop(0, early, one_slot, 0)

    for copy in peer_copies:
        copy.wait_recv()

    def interpolate(m, carry):
        at = pl.ds(pl.multiple_of(m * LANES, LANES), LANES)
        source = src_ref[:, at]
        weight = weight_ref[:, at]
        from_peer = lax.shift_right_arithmetic(source, 7)
        from_slot = source & (LANES - 1)

        def one_peer(p, acc):
            here = from_peer == p
            return tuple(
                jnp.where(here, lookup(in_buf[p, f : f + 1, :], from_slot), acc[f]) for f in range(4)
            )

        acc = tuple(jnp.zeros((8, LANES), jnp.float32) for _ in range(4))
        if peers <= 8:
            for p in range(peers):
                acc = one_peer(p, acc)
        else:
            acc = lax.fori_loop(0, peers, one_peer, acc)
        for f in range(4):
            value = -jnp.sum(weight * acc[f], axis=0, keepdims=True)
            big = value.astype(jnp.bfloat16)
            rest = (value - big.astype(jnp.float32)).astype(jnp.bfloat16)
            hit = by_lane[:, at]
            to = pl.ds(pl.multiple_of(ghosts + m * LANES, LANES), LANES)
            spread[LANES * f : LANES * (f + 1), at] = hit * jnp.broadcast_to(big, hit.shape)
            spread[LANES * f : LANES * (f + 1), to] = hit * jnp.broadcast_to(rest, hit.shape)
        return carry

    lax.fori_loop(0, chunks, interpolate, 0, unroll=4 if peers <= 8 else 1)

    stored = lax.dot_general(by_row[...], spread[...], last_dims, preferred_element_type=jnp.float32)
    for f in range(4):
        value = stored[:, LANES * f : LANES * (f + 1)].reshape(cx, cy, LANES)
        filled[f] = jnp.where(is_ghost[...] > 0.5, value, fields[f])

    low_high = ((a, nx), (b, ny), (c, nz))

    def exists(axis, side):
        index, count = low_high[axis]
        return index > 0 if side == 0 else index < count - 1

    def beside(axis, side):
        place = [a, b, c]
        place[axis] = place[axis] + (1 if side else -1)
        return tuple(place)

    def halo_copy(axis, side, arrives):
        if axis == 0:
            source = filled.at[:, 0:2] if side == 0 else filled.at[:, cx - 2 : cx]
        else:
            source = (pack_y, pack_z)[axis - 1].at[side]
        end = side if arrives else 1 - side
        return pltpu.make_async_remote_copy(
            src_ref=source,
            dst_ref=(halo_x, halo_y, halo_z)[axis].at[end],
            send_sem=halo_send.at[2 * axis + side],
            recv_sem=halo_recv.at[2 * axis + end],
            device_id=beside(axis, side),
            device_id_type=MESH,
        )

    def send_halo(axis):
        for side in range(2):
            @pl.when(exists(axis, side))
            def _():
                halo_copy(axis, side, False).start()

    def wait_halo(axis):
        for side in range(2):
            @pl.when(exists(axis, side))
            def _():
                halo_copy(axis, side, True).wait_recv()

    send_halo(0)
    core_copy = pltpu.make_async_copy(filled, core, core_sem)
    core_copy.start()
    for f in range(4):
        for i in range(cx):
            at = 2 * (f * cx + i)
            pack_y[0, at : at + 2, :] = filled[f, i, 0:2, :]
            pack_y[1, at : at + 2, :] = filled[f, i, cy - 2 : cy, :]
    send_halo(1)
    planes = LANES // cy
    blocks = cx // planes
    for f in range(4):
        for g in range(blocks):
            block = filled[f, planes * g : planes * (g + 1)].reshape(LANES, LANES)
            across = block.T
            at = 2 * (f * blocks + g)
            pack_z[0, at : at + 2, :] = across[0:2, :]
            pack_z[1, at : at + 2, :] = across[LANES - 2 : LANES, :]
    send_halo(2)

    lax.fori_loop(early, slots, one_slot, 0)

    def place(i, carry):
        for jb in range(rows_y):
            wall = jnp.full((8, LANES), dist_cap, jnp.float32)
            for s in range(slots):
                wall = jnp.where(tile_of[s] == i * per_row + jb, dist[s], wall)
            wall_ref[i, 8 * jb : 8 * jb + 8, :] = wall
        return carry

    lax.fori_loop(0, cx, place, 0)
    wall_copy = pltpu.make_async_copy(wall_ref, wall_out, wall_sem)
    wall_copy.start()

    for axis in range(3):
        wait_halo(axis)
    for copy in peer_copies + point_copies:
        copy.wait_send()
    for axis in range(3):
        for side in range(2):
            @pl.when(exists(axis, side))
            def _():
                halo_copy(axis, side, False).wait_send()

    core_copy.wait()
    wall_copy.wait()


def step_kernel(
    sizes,
    core,
    halo_x,
    halo_y,
    halo_z,
    wall_hbm,
    fluid_hbm,
    new_vel,
    new_nu,
    wall_out,
    padded,
    got_y,
    got_z,
    wall_ref,
    fluid_ref,
    turn,
    edge_z,
    vel_ref,
    nu_ref,
    load,
    halo_load,
    wall_sem,
    vel_sem,
    nu_sem,
):
    cx, cy, _ = wall_ref.shape
    rows_y = cy // 8
    planes = LANES // cy
    blocks = cx // planes
    lane = lax.broadcasted_iota(jnp.int32, (8, LANES), 1)
    place = [lax.axis_index(name) for name in ("gx", "gy", "gz")]
    margin_x = (padded.at[:, 0:2, 8 : 8 + cy, :], padded.at[:, cx + 2 : cx + 4, 8 : 8 + cy, :])
    targets = (margin_x, (got_y.at[0], got_y.at[1]), (got_z.at[0], got_z.at[1]))

    def exists(axis, side):
        return place[axis] > 0 if side == 0 else place[axis] < sizes[axis] - 1

    def halo_copy(axis, side):
        source = (halo_x, halo_y, halo_z)[axis].at[side]
        return pltpu.make_async_copy(source, targets[axis][side], halo_load.at[2 * axis + side])

    core_copy = pltpu.make_async_copy(core, padded.at[:, 2 : cx + 2, 8 : 8 + cy, :], load.at[0])
    wall_copy = pltpu.make_async_copy(wall_hbm, wall_ref, load.at[1])
    fluid_copy = pltpu.make_async_copy(fluid_hbm, fluid_ref, load.at[2])
    for axis in (2, 1, 0):
        for side in range(2):
            @pl.when(exists(axis, side))
            def _():
                halo_copy(axis, side).start()

    core_copy.start()
    wall_copy.start()
    fluid_copy.start()
    for axis in (2, 1, 0):
        for side in range(2):
            target = targets[axis][side]

            @pl.when(jnp.logical_not(exists(axis, side)))
            def _():
                target[...] = jnp.zeros(target.shape, jnp.float32)

    for axis in (2, 1, 0):
        for side in range(2):
            @pl.when(exists(axis, side))
            def _():
                halo_copy(axis, side).wait()

    for f in range(4):
        for g in range(blocks):
            at = 2 * (f * blocks + g)
            turn[f * blocks + g, 0:2, :] = got_z[1, at : at + 2, :]
            turn[f * blocks + g, LANES - 2 : LANES, :] = got_z[0, at : at + 2, :]
            edge_z[f, planes * g : planes * (g + 1), :, :] = turn[f * blocks + g].T.reshape(planes, cy, LANES)
    for f in range(4):
        for i in range(cx):
            at = 2 * (f * cx + i)
            padded[f, i + 2, 6:8, :] = got_y[0, at : at + 2, :]
            padded[f, i + 2, 8 + cy : 10 + cy, :] = got_y[1, at : at + 2, :]

    core_copy.wait()
    wall_copy.wait()
    fluid_copy.wait()
    show_wall = pltpu.make_async_copy(wall_ref, wall_out, wall_sem)
    show_wall.start()

    def plane_copies(i):
        return (
            pltpu.make_async_copy(vel_ref.at[:, i], new_vel.at[:, i], vel_sem.at[i]),
            pltpu.make_async_copy(nu_ref.at[i], new_nu.at[i], nu_sem.at[i]),
        )

    def advance(i, carry):
        for jb in range(rows_y):
            advance_rows(i, jb)
        for copy in plane_copies(i):
            copy.start()
        return carry

    def advance_rows(i, jb):
        center, gradient, laplace = [], [[], [], []], []

        def slope(m2, m1, p1, p2):
            return ((m2 - p2) + 8.0 * (p1 - m1)) * (1.0 / 12.0)

        for f in range(4):
            begin = 8 + 8 * jb
            mid = padded[f, i + 2, begin : begin + 8, :]
            x = [padded[f, i + 2 + h, begin : begin + 8, :] for h in (-2, -1, 1, 2)]
            y = [padded[f, i + 2, begin + h : begin + h + 8, :] for h in (-2, -1, 1, 2)]
            rim = edge_z[f, i, 8 * jb : 8 * jb + 8, :]
            z = [
                pltpu.roll(jnp.where(lane >= LANES - 2, rim, mid), 2, 1),
                pltpu.roll(jnp.where(lane >= LANES - 1, rim, mid), 1, 1),
                pltpu.roll(jnp.where(lane < 1, rim, mid), LANES - 1, 1),
                pltpu.roll(jnp.where(lane < 2, rim, mid), LANES - 2, 1),
            ]
            center.append(mid)
            for e, line in enumerate((x, y, z)):
                gradient[e].append(slope(*line))
            laplace.append(((x[1] + x[2]) + (y[1] + y[2])) + ((z[1] + z[2]) - 6.0 * mid))
        u, v, w, working = center
        curl_x = gradient[1][2] - gradient[2][1]
        curl_y = gradient[2][0] - gradient[0][2]
        curl_z = gradient[0][1] - gradient[1][0]
        rate = jnp.maximum(jnp.sqrt(curl_x * curl_x + curl_y * curl_y + curl_z * curl_z), floor_rate)
        positive = jnp.maximum(working, 0.0)
        chi = positive * (1.0 / viscosity)
        chi_cubed = chi * chi * chi
        diffusion = viscosity + positive * chi_cubed / (chi_cubed + visc_coef**3)
        wall = wall_ref[i, 8 * jb : 8 * jb + 8, :]
        arg = (8.0 * diffusion) / (rate * (karman * karman) * (wall * wall))
        shield = 1.0 - jnp.tanh(arg * arg * arg)
        length = wall - shield * jnp.maximum(wall - des_coef, 0.0)
        scale = time_step * fluid_ref[i, 8 * jb : 8 * jb + 8, :].astype(jnp.float32)
        for f in range(4):
            convect = u * gradient[0][f] + v * gradient[1][f] + w * gradient[2][f]
            if f < 3:
                change = diffusion * laplace[f] - convect
                vel_ref[f, i, 8 * jb : 8 * jb + 8, :] = center[f] + scale * change
            else:
                squares = (
                    gradient[0][3] * gradient[0][3]
                    + gradient[1][3] * gradient[1][3]
                    + gradient[2][3] * gradient[2][3]
                )
                change = (
                    sigma_inv * ((viscosity + positive) * laplace[3] + grad_coef * squares)
                    - convect
                    + prod_coef * rate * working
                    - wall_coef * working * jnp.abs(working) / (length * length)
                )
                nu_ref[i, 8 * jb : 8 * jb + 8, :] = working + scale * change

    lax.fori_loop(0, cx, advance, 0)

    def finish(i, carry):
        for copy in plane_copies(i):
            copy.wait()
        return carry

    lax.fori_loop(0, cx, finish, 0)
    show_wall.wait()


def on_device(
    velocity,
    nu_tilde,
    fluid_cells,
    surface,
    pitch_angle,
    near_tiles,
    send_rows,
    ghost_cell,
    ghost_src,
    ghost_weight,
):
    nx, ny, nz = (lax.axis_size(name) for name in ("gx", "gy", "gz"))
    peers = nx * nz
    _, cx, cy, cz = velocity.shape
    ghosts = ghost_cell.shape[-1]
    points_dev = surface.shape[-1]
    slots = near_tiles.shape[-1]
    hbm = pl.BlockSpec(memory_space=pltpu.HBM)
    f32, i32 = jnp.float32, jnp.int32
    limit = 60 * 1024 * 1024
    edge = 8 * cx * cy // LANES
    work = pl.pallas_call(
        functools.partial(fill_kernel, (nx, ny, nz)),
        out_shape=(
            jax.ShapeDtypeStruct((4, cx, cy, cz), f32),
            jax.ShapeDtypeStruct((2, 4, 2, cy, cz), f32),
            jax.ShapeDtypeStruct((2, 8 * cx, cz), f32),
            jax.ShapeDtypeStruct((2, edge, LANES), f32),
            jax.ShapeDtypeStruct((cx, cy, cz), f32),
        ),
        in_specs=[hbm] * 9,
        out_specs=(hbm,) * 5,
        scratch_shapes=[
            pltpu.VMEM((4, cx, cy, cz), f32),
            pltpu.VMEM((cx, cy, cz), f32),
            pltpu.VMEM((4, cx, cy, cz), f32),
            pltpu.VMEM((3, 1, points_dev), f32),
            pltpu.SMEM((1,), f32),
            pltpu.VMEM((1, slots), i32),
            pltpu.VMEM((peers, LANES), i32),
            pltpu.VMEM((1, ghosts), i32),
            pltpu.VMEM((8, ghosts), i32),
            pltpu.VMEM((8, ghosts), f32),
            pltpu.VMEM((peers, 4, LANES), f32),
            pltpu.VMEM((peers, 4, LANES), f32),
            pltpu.VMEM((ny, 8, points_dev), f32),
            pltpu.VMEM((cx, cy, LANES), f32),
            pltpu.VMEM((4 * LANES, 2 * ghosts), jnp.bfloat16),
            pltpu.VMEM((2 * cx * cy, peers * LANES), jnp.bfloat16),
            pltpu.VMEM((4 * LANES, 2 * cx * cy), jnp.bfloat16),
            pltpu.VMEM((cx * cy, 2 * ghosts), jnp.bfloat16),
            pltpu.VMEM((LANES, ghosts), jnp.bfloat16),
            pltpu.VMEM((2, 8 * cx, cz), f32),
            pltpu.VMEM((2, edge, LANES), f32),
            pltpu.VMEM((ny * points_dev, cz), f32),
            pltpu.VMEM((ny * points_dev, cz), f32),
            pltpu.VMEM((ny * points_dev, cz), f32),
            pltpu.VMEM((slots, TY, cz), f32),
            pltpu.VMEM((slots, TY, cz), i32),
            pltpu.SemaphoreType.DMA,
            pltpu.SemaphoreType.DMA,
            pltpu.SemaphoreType.DMA((9,)),
            pltpu.SemaphoreType.DMA((peers,)),
            pltpu.SemaphoreType.DMA((peers,)),
            pltpu.SemaphoreType.DMA((ny,)),
            pltpu.SemaphoreType.DMA((ny,)),
            pltpu.SemaphoreType.DMA((6,)),
            pltpu.SemaphoreType.DMA((6,)),
        ],
        compiler_params=pltpu.CompilerParams(
            collective_id=0, has_side_effects=True, vmem_limit_bytes=limit
        ),
    )(
        velocity,
        nu_tilde,
        jnp.transpose(surface, (0, 2, 1, 3))[0],
        pitch_angle,
        near_tiles[0, 0],
        send_rows[0, 0, 0],
        ghost_cell[0, 0],
        ghost_src[0, 0, 0],
        ghost_weight[0, 0, 0],
    )
    return pl.pallas_call(
        functools.partial(step_kernel, (nx, ny, nz)),
        out_shape=(
            jax.ShapeDtypeStruct(velocity.shape, f32),
            jax.ShapeDtypeStruct(nu_tilde.shape, f32),
            jax.ShapeDtypeStruct(nu_tilde.shape, f32),
        ),
        in_specs=[hbm] * 6,
        out_specs=(hbm,) * 3,
        scratch_shapes=[
            pltpu.VMEM((4, cx + 4, cy + 16, cz), f32),
            pltpu.VMEM((2, 8 * cx, cz), f32),
            pltpu.VMEM((2, edge, LANES), f32),
            pltpu.VMEM((cx, cy, cz), f32),
            pltpu.VMEM((cx, cy, cz), i32),
            pltpu.VMEM((4 * cx * cy // LANES, LANES, LANES), f32),
            pltpu.VMEM((4, cx, cy, cz), f32),
            pltpu.VMEM(velocity.shape, f32),
            pltpu.VMEM(nu_tilde.shape, f32),
            pltpu.SemaphoreType.DMA((3,)),
            pltpu.SemaphoreType.DMA((6,)),
            pltpu.SemaphoreType.DMA,
            pltpu.SemaphoreType.DMA((cx,)),
            pltpu.SemaphoreType.DMA((cx,)),
        ],
        compiler_params=pltpu.CompilerParams(vmem_limit_bytes=limit),
    )(*work, fluid_cells)


def solution(mesh):
    in_specs = (
        P(None, "gx", "gy", "gz"),
        P("gx", "gy", "gz"),
        P("gx", "gy", "gz"),
        P("gx", "gz", None, "gy"),
        P(),
        P("gx", "gy", "gz", None),
        P("gx", "gy", "gz", None, None),
        P("gx", "gy", "gz", None),
        P("gx", "gy", "gz", None, None),
        P("gx", "gy", "gz", None, None),
    )
    out_specs = (P(None, "gx", "gy", "gz"), P("gx", "gy", "gz"), P("gx", "gy", "gz"))
    return jax.shard_map(
        on_device, mesh=mesh, in_specs=in_specs, out_specs=out_specs, check_vma=False
    )
```

```python
import functools

import jax
import jax.numpy as jnp
from jax import lax
from jax.experimental import pallas as pl
from jax.experimental.pallas import tpu as pltpu
from jax.sharding import PartitionSpec as P

MESH = pl.DeviceIdType.MESH
TY = 8
LANES = 128

viscosity = 0.2
prod_coef = 0.1355
grad_coef = 0.622
sigma_inv = 1.5
karman = 0.41
visc_coef = 7.1
wall_coef = prod_coef / (karman * karman) + (1.0 + grad_coef) * sigma_inv
des_coef = 0.65
floor_rate = 0.3
dist_eps = 0.25
dist_cap = 8.0
time_step = 0.05


def lookup(row, lanes):
    table = jnp.broadcast_to(row, lanes.shape)
    return lax.gather(
        table,
        lanes[:, :, None],
        lax.GatherDimensionNumbers(
            offset_dims=(),
            collapsed_slice_dims=(1,),
            start_index_map=(1,),
            operand_batching_dims=(0,),
            start_indices_batching_dims=(0,),
        ),
        slice_sizes=(1, 1),
        mode=lax.GatherScatterMode.PROMISE_IN_BOUNDS,
    )


def fill_kernel(
    sizes,
    vel_hbm,
    nu_hbm,
    surf_hbm,
    pitch_hbm,
    tiles_hbm,
    rows_hbm,
    cell_hbm,
    src_hbm,
    weight_hbm,
    core,
    halo_x,
    halo_y,
    halo_z,
    wall_out,
    filled,
    wall_ref,
    fields,
    surf_ref,
    pitch_ref,
    tiles_ref,
    rows_ref,
    cell_ref,
    src_ref,
    weight_ref,
    out_buf,
    in_buf,
    points,
    is_ghost,
    spread,
    choose,
    parts,
    by_row,
    by_lane,
    pack_y,
    pack_z,
    flat_x,
    flat_y,
    flat_z2,
    dist,
    tile_of,
    core_sem,
    wall_sem,
    load,
    peer_send,
    peer_recv,
    point_send,
    point_recv,
    halo_send,
    halo_recv,
):
    pairs = (
        (pitch_hbm, pitch_ref),
        (surf_hbm, surf_ref),
        (rows_hbm, rows_ref),
        (vel_hbm, fields.at[0:3]),
        (nu_hbm, fields.at[3]),
        (cell_hbm, cell_ref),
        (src_hbm, src_ref),
        (weight_hbm, weight_ref),
        (tiles_hbm, tiles_ref),
    )
    loads = [pltpu.make_async_copy(x, y, load.at[i]) for i, (x, y) in enumerate(pairs)]
    for copy in loads:
        copy.start()

    nx, ny, nz = sizes
    peers = nx * nz
    _, cx, cy, cz = vel_hbm.shape
    rows_y = cy // 8
    chunks = cell_hbm.shape[1] // LANES
    a, b, c = (lax.axis_index(name) for name in ("gx", "gy", "gz"))
    me = a * nz + c
    lane = lax.broadcasted_iota(jnp.int32, (8, LANES), 1)
    slots = tiles_hbm.shape[1]
    per_row = cy // TY

    def peer_of(d):
        other = lax.rem(me + d, peers)
        return other, (lax.div(other, nz), b, lax.rem(other, nz))

    def column_of(d):
        other = lax.rem(b + d, ny)
        return other, (a, other, c)

    barrier = pltpu.get_barrier_semaphore()
    for d in range(1, peers):
        pl.semaphore_signal(barrier, inc=1, device_id=peer_of(d)[1], device_id_type=MESH)
    for d in range(1, ny):
        pl.semaphore_signal(barrier, inc=1, device_id=column_of(d)[1], device_id_type=MESH)

    for copy in loads[0:2]:
        copy.wait()
    angle = jnp.full((1, LANES), pitch_ref[0], jnp.float32)
    cosine, sine = jnp.cos(angle), jnp.sin(angle)
    px, py, pz = surf_ref[0], surf_ref[1], surf_ref[2]
    points[b] = jnp.concatenate(
        [cosine * px + sine * pz, py, cosine * pz - sine * px, jnp.zeros((5, LANES), jnp.float32)], axis=0
    )

    pl.semaphore_wait(barrier, peers - 1 + ny - 1)

    def point_copy(d):
        return pltpu.make_async_remote_copy(
            src_ref=points.at[b],
            dst_ref=points.at[b],
            send_sem=point_send.at[d],
            recv_sem=point_recv.at[d],
            device_id=column_of(d)[1],
            device_id_type=MESH,
        )

    point_copies = [point_copy(d) for d in range(1, ny)]
    for copy in point_copies:
        copy.start()

    cells_hi = cx * cy
    loads[2].wait()
    row_number = lax.broadcasted_iota(jnp.int32, (cells_hi, LANES), 0)
    lane_number = lax.broadcasted_iota(jnp.int32, (LANES, 2 * LANES), 0)
    for p in range(peers):
        wanted = lax.shift_right_arithmetic(rows_ref[p : p + 1, :], 7)
        hit = jnp.where(row_number == wanted, 1.0, 0.0).astype(jnp.bfloat16)
        choose[0:cells_hi, LANES * p : LANES * (p + 1)] = hit
        choose[cells_hi : 2 * cells_hi, LANES * p : LANES * (p + 1)] = hit

    for copy in loads[3:5]:
        copy.wait()
    for f in range(4):
        across = fields[f].reshape(cells_hi, LANES).T
        big = across.astype(jnp.bfloat16)
        rest = (across - big.astype(jnp.float32)).astype(jnp.bfloat16)
        parts[LANES * f : LANES * (f + 1), 0:cells_hi] = big
        parts[LANES * f : LANES * (f + 1), cells_hi : 2 * cells_hi] = rest

    def pick(k, carry):
        at = pl.multiple_of(k * 2 * LANES, 2 * LANES)
        found = jnp.dot(
            parts[...], choose[:, pl.ds(at, 2 * LANES)], preferred_element_type=jnp.float32
        )
        both = jnp.concatenate([rows_ref[pl.ds(2 * k, 1), :], rows_ref[pl.ds(2 * k + 1, 1), :]], axis=1)
        here = lane_number == (both & (LANES - 1))
        for f in range(4):
            row = jnp.sum(
                jnp.where(here, found[LANES * f : LANES * (f + 1), :], 0.0), axis=0, keepdims=True
            )
            out_buf[2 * k, f : f + 1, :] = row[:, 0:LANES]
            out_buf[2 * k + 1, f : f + 1, :] = row[:, LANES : 2 * LANES]
        return carry

    lax.fori_loop(0, peers // 2, pick, 0, unroll=peers <= 8)

    def peer_copy(d):
        other, device = peer_of(d)
        return pltpu.make_async_remote_copy(
            src_ref=out_buf.at[other],
            dst_ref=in_buf.at[me],
            send_sem=peer_send.at[d],
            recv_sem=peer_recv.at[d],
            device_id=device,
            device_id_type=MESH,
        )

    peer_copies = [peer_copy(d) for d in range(1, peers)]
    for copy in peer_copies:
        copy.start()
    in_buf[me] = out_buf[me]

    for copy in loads[5:]:
        copy.wait()

    for copy in point_copies:
        copy.wait_recv()
    deep = (lax.broadcasted_iota(jnp.int32, (LANES, LANES), 1).astype(jnp.float32) + 0.5) - 0.5 * cz
    for g in range(ny):
        at = slice(LANES * g, LANES * (g + 1))
        flat_x[at, :] = jnp.broadcast_to(points[g, 0:1, :], (LANES, LANES)).T
        flat_y[at, :] = jnp.broadcast_to(points[g, 1:2, :], (LANES, LANES)).T
        step_z = deep - jnp.broadcast_to(points[g, 2:3, :], (LANES, LANES)).T
        flat_z2[at, :] = step_z * step_z

    for s in range(slots):
        tile_of[s] = jnp.broadcast_to(tiles_ref[0:1, s : s + 1], (8, LANES))

    def one_slot(s, carry):
        tile = jnp.maximum(tile_of[s], 0)
        at_x = lax.div(tile, per_row).astype(jnp.float32) + (0.5 - 0.5 * cx)
        first = lax.rem(tile, per_row) * TY + b * cy
        at_y = first.astype(jnp.float32) + (0.5 - 0.5 * (ny * cy))

        def some_points(k, best):
            for u in range(16):
                at = pl.ds(pl.multiple_of(k * LANES, LANES) + 8 * u, 8)
                step_x = at_x - flat_x[at, :]
                step_y = at_y - flat_y[at, :]
                value = (step_x * step_x + step_y * step_y) + flat_z2[at, :]
                twice = step_y + step_y
                new = [jnp.minimum(best[0], value)]
                for r in range(1, TY):
                    value = value + twice
                    new.append(jnp.minimum(best[r], value))
                best = tuple(new)
            return best

        start = tuple(jnp.full((8, LANES), jnp.inf, jnp.float32) for _ in range(TY))
        best = lax.fori_loop(0, ny, some_points, start)
        least = jnp.concatenate(
            [jnp.min(x, axis=0, keepdims=True) + float(r * r) for r, x in enumerate(best)], axis=0
        )
        dist[s] = jnp.minimum(jnp.sqrt(least + dist_eps), dist_cap)
        return carry

    ghosts = cell_ref.shape[1]
    cells = cell_ref[...]
    row_id = lax.broadcasted_iota(jnp.int32, (cells_hi, ghosts), 0)
    lane_id = lax.broadcasted_iota(jnp.int32, (LANES, ghosts), 0)
    hit_row = jnp.where(row_id == lax.shift_right_arithmetic(cells, 7), 1.0, 0.0).astype(jnp.bfloat16)
    by_row[:, 0:ghosts] = hit_row
    by_row[:, ghosts : 2 * ghosts] = hit_row
    by_lane[...] = jnp.where(lane_id == (cells & (LANES - 1)), 1.0, 0.0).astype(jnp.bfloat16)
    last_dims = (((1,), (1,)), ((), ()))
    is_ghost[...] = lax.dot_general(
        by_row[:, 0:ghosts], by_lane[...], last_dims, preferred_element_type=jnp.float32
    ).reshape(cx, cy, LANES)

    early = slots // 4
    lax.fori_loop(0, early, one_slot, 0)

    for copy in peer_copies:
        copy.wait_recv()

    def interpolate(m, carry):
        at = pl.ds(pl.multiple_of(m * LANES, LANES), LANES)
        source = src_ref[:, at]
        weight = weight_ref[:, at]
        from_peer = lax.shift_right_arithmetic(source, 7)
        from_slot = source & (LANES - 1)

        def one_peer(p, acc):
            here = from_peer == p
            return tuple(
                jnp.where(here, lookup(in_buf[p, f : f + 1, :], from_slot), acc[f]) for f in range(4)
            )

        acc = tuple(jnp.zeros((8, LANES), jnp.float32) for _ in range(4))
        if peers <= 8:
            for p in range(peers):
                acc = one_peer(p, acc)
        else:
            acc = lax.fori_loop(0, peers, one_peer, acc)
        for f in range(4):
            value = -jnp.sum(weight * acc[f], axis=0, keepdims=True)
            big = value.astype(jnp.bfloat16)
            rest = (value - big.astype(jnp.float32)).astype(jnp.bfloat16)
            hit = by_lane[:, at]
            to = pl.ds(pl.multiple_of(ghosts + m * LANES, LANES), LANES)
            spread[LANES * f : LANES * (f + 1), at] = hit * jnp.broadcast_to(big, hit.shape)
            spread[LANES * f : LANES * (f + 1), to] = hit * jnp.broadcast_to(rest, hit.shape)
        return carry

    lax.fori_loop(0, chunks, interpolate, 0, unroll=4 if peers <= 8 else 1)

    stored = lax.dot_general(by_row[...], spread[...], last_dims, preferred_element_type=jnp.float32)
    for f in range(4):
        value = stored[:, LANES * f : LANES * (f + 1)].reshape(cx, cy, LANES)
        filled[f] = jnp.where(is_ghost[...] > 0.5, value, fields[f])

    low_high = ((a, nx), (b, ny), (c, nz))

    def exists(axis, side):
        index, count = low_high[axis]
        return index > 0 if side == 0 else index < count - 1

    def beside(axis, side):
        place = [a, b, c]
        place[axis] = place[axis] + (1 if side else -1)
        return tuple(place)

    def halo_copy(axis, side, arrives):
        if axis == 0:
            source = filled.at[:, 0:2] if side == 0 else filled.at[:, cx - 2 : cx]
        else:
            source = (pack_y, pack_z)[axis - 1].at[side]
        end = side if arrives else 1 - side
        return pltpu.make_async_remote_copy(
            src_ref=source,
            dst_ref=(halo_x, halo_y, halo_z)[axis].at[end],
            send_sem=halo_send.at[2 * axis + side],
            recv_sem=halo_recv.at[2 * axis + end],
            device_id=beside(axis, side),
            device_id_type=MESH,
        )

    def send_halo(axis):
        for side in range(2):
            @pl.when(exists(axis, side))
            def _():
                halo_copy(axis, side, False).start()

    def wait_halo(axis):
        for side in range(2):
            @pl.when(exists(axis, side))
            def _():
                halo_copy(axis, side, True).wait_recv()

    send_halo(0)
    core_copy = pltpu.make_async_copy(filled, core, core_sem)
    core_copy.start()
    for f in range(4):
        for i in range(cx):
            at = 2 * (f * cx + i)
            pack_y[0, at : at + 2, :] = filled[f, i, 0:2, :]
            pack_y[1, at : at + 2, :] = filled[f, i, cy - 2 : cy, :]
    send_halo(1)
    planes = LANES // cy
    blocks = cx // planes
    for f in range(4):
        for g in range(blocks):
            block = filled[f, planes * g : planes * (g + 1)].reshape(LANES, LANES)
            across = block.T
            at = 2 * (f * blocks + g)
            pack_z[0, at : at + 2, :] = across[0:2, :]
            pack_z[1, at : at + 2, :] = across[LANES - 2 : LANES, :]
    send_halo(2)

    lax.fori_loop(early, slots, one_slot, 0)

    def place(i, carry):
        for jb in range(rows_y):
            wall = jnp.full((8, LANES), dist_cap, jnp.float32)
            for s in range(slots):
                wall = jnp.where(tile_of[s] == i * per_row + jb, dist[s], wall)
            wall_ref[i, 8 * jb : 8 * jb + 8, :] = wall
        return carry

    lax.fori_loop(0, cx, place, 0)
    wall_copy = pltpu.make_async_copy(wall_ref, wall_out, wall_sem)
    wall_copy.start()

    for axis in range(3):
        wait_halo(axis)
    for copy in peer_copies + point_copies:
        copy.wait_send()
    for axis in range(3):
        for side in range(2):
            @pl.when(exists(axis, side))
            def _():
                halo_copy(axis, side, False).wait_send()

    core_copy.wait()
    wall_copy.wait()


def step_kernel(
    sizes,
    core,
    halo_x,
    halo_y,
    halo_z,
    wall_hbm,
    fluid_hbm,
    new_vel,
    new_nu,
    wall_out,
    padded,
    got_y,
    got_z,
    wall_ref,
    fluid_ref,
    turn,
    edge_z,
    vel_ref,
    nu_ref,
    load,
    halo_load,
    wall_sem,
    vel_sem,
    nu_sem,
):
    cx, cy, _ = wall_ref.shape
    rows_y = cy // 8
    planes = LANES // cy
    blocks = cx // planes
    lane = lax.broadcasted_iota(jnp.int32, (8, LANES), 1)
    place = [lax.axis_index(name) for name in ("gx", "gy", "gz")]
    margin_x = (padded.at[:, 0:2, 8 : 8 + cy, :], padded.at[:, cx + 2 : cx + 4, 8 : 8 + cy, :])
    targets = (margin_x, (got_y.at[0], got_y.at[1]), (got_z.at[0], got_z.at[1]))

    def exists(axis, side):
        return place[axis] > 0 if side == 0 else place[axis] < sizes[axis] - 1

    def halo_copy(axis, side):
        source = (halo_x, halo_y, halo_z)[axis].at[side]
        return pltpu.make_async_copy(source, targets[axis][side], halo_load.at[2 * axis + side])

    core_copy = pltpu.make_async_copy(core, padded.at[:, 2 : cx + 2, 8 : 8 + cy, :], load.at[0])
    wall_copy = pltpu.make_async_copy(wall_hbm, wall_ref, load.at[1])
    fluid_copy = pltpu.make_async_copy(fluid_hbm, fluid_ref, load.at[2])
    for axis in (2, 1, 0):
        for side in range(2):
            @pl.when(exists(axis, side))
            def _():
                halo_copy(axis, side).start()

    core_copy.start()
    wall_copy.start()
    fluid_copy.start()
    for axis in (2, 1, 0):
        for side in range(2):
            target = targets[axis][side]

            @pl.when(jnp.logical_not(exists(axis, side)))
            def _():
                target[...] = jnp.zeros(target.shape, jnp.float32)

    for axis in (2, 1, 0):
        for side in range(2):
            @pl.when(exists(axis, side))
            def _():
                halo_copy(axis, side).wait()

    for f in range(4):
        for g in range(blocks):
            at = 2 * (f * blocks + g)
            turn[f * blocks + g, 0:2, :] = got_z[1, at : at + 2, :]
            turn[f * blocks + g, LANES - 2 : LANES, :] = got_z[0, at : at + 2, :]
            edge_z[f, planes * g : planes * (g + 1), :, :] = turn[f * blocks + g].T.reshape(planes, cy, LANES)
    for f in range(4):
        for i in range(cx):
            at = 2 * (f * cx + i)
            padded[f, i + 2, 6:8, :] = got_y[0, at : at + 2, :]
            padded[f, i + 2, 8 + cy : 10 + cy, :] = got_y[1, at : at + 2, :]

    core_copy.wait()
    wall_copy.wait()
    fluid_copy.wait()
    show_wall = pltpu.make_async_copy(wall_ref, wall_out, wall_sem)
    show_wall.start()

    def plane_copies(i):
        return (
            pltpu.make_async_copy(vel_ref.at[:, i], new_vel.at[:, i], vel_sem.at[i]),
            pltpu.make_async_copy(nu_ref.at[i], new_nu.at[i], nu_sem.at[i]),
        )

    def advance(i, carry):
        for jb in range(rows_y):
            advance_rows(i, jb)
        for copy in plane_copies(i):
            copy.start()
        return carry

    def advance_rows(i, jb):
        center, gradient, laplace = [], [[], [], []], []

        def slope(m2, m1, p1, p2):
            return ((m2 - p2) + 8.0 * (p1 - m1)) * (1.0 / 12.0)

        for f in range(4):
            begin = 8 + 8 * jb
            mid = padded[f, i + 2, begin : begin + 8, :]
            x = [padded[f, i + 2 + h, begin : begin + 8, :] for h in (-2, -1, 1, 2)]
            y = [padded[f, i + 2, begin + h : begin + h + 8, :] for h in (-2, -1, 1, 2)]
            rim = edge_z[f, i, 8 * jb : 8 * jb + 8, :]
            z = [
                pltpu.roll(jnp.where(lane >= LANES - 2, rim, mid), 2, 1),
                pltpu.roll(jnp.where(lane >= LANES - 1, rim, mid), 1, 1),
                pltpu.roll(jnp.where(lane < 1, rim, mid), LANES - 1, 1),
                pltpu.roll(jnp.where(lane < 2, rim, mid), LANES - 2, 1),
            ]
            center.append(mid)
            for e, line in enumerate((x, y, z)):
                gradient[e].append(slope(*line))
            laplace.append(((x[1] + x[2]) + (y[1] + y[2])) + ((z[1] + z[2]) - 6.0 * mid))
        u, v, w, working = center
        curl_x = gradient[1][2] - gradient[2][1]
        curl_y = gradient[2][0] - gradient[0][2]
        curl_z = gradient[0][1] - gradient[1][0]
        rate = jnp.maximum(jnp.sqrt(curl_x * curl_x + curl_y * curl_y + curl_z * curl_z), floor_rate)
        positive = jnp.maximum(working, 0.0)
        chi = positive * (1.0 / viscosity)
        chi_cubed = chi * chi * chi
        diffusion = viscosity + positive * chi_cubed / (chi_cubed + visc_coef**3)
        wall = wall_ref[i, 8 * jb : 8 * jb + 8, :]
        arg = (8.0 * diffusion) / (rate * (karman * karman) * (wall * wall))
        shield = 1.0 - jnp.tanh(arg * arg * arg)
        length = wall - shield * jnp.maximum(wall - des_coef, 0.0)
        scale = time_step * fluid_ref[i, 8 * jb : 8 * jb + 8, :].astype(jnp.float32)
        for f in range(4):
            convect = u * gradient[0][f] + v * gradient[1][f] + w * gradient[2][f]
            if f < 3:
                change = diffusion * laplace[f] - convect
                vel_ref[f, i, 8 * jb : 8 * jb + 8, :] = center[f] + scale * change
            else:
                squares = (
                    gradient[0][3] * gradient[0][3]
                    + gradient[1][3] * gradient[1][3]
                    + gradient[2][3] * gradient[2][3]
                )
                change = (
                    sigma_inv * ((viscosity + positive) * laplace[3] + grad_coef * squares)
                    - convect
                    + prod_coef * rate * working
                    - wall_coef * working * jnp.abs(working) / (length * length)
                )
                nu_ref[i, 8 * jb : 8 * jb + 8, :] = working + scale * change

    lax.fori_loop(0, cx, advance, 0)

    def finish(i, carry):
        for copy in plane_copies(i):
            copy.wait()
        return carry

    lax.fori_loop(0, cx, finish, 0)
    show_wall.wait()


def on_device(
    velocity,
    nu_tilde,
    fluid_cells,
    surface,
    pitch_angle,
    near_tiles,
    send_rows,
    ghost_cell,
    ghost_src,
    ghost_weight,
):
    nx, ny, nz = (lax.axis_size(name) for name in ("gx", "gy", "gz"))
    peers = nx * nz
    _, cx, cy, cz = velocity.shape
    ghosts = ghost_cell.shape[-1]
    points_dev = surface.shape[-1]
    slots = near_tiles.shape[-1]
    hbm = pl.BlockSpec(memory_space=pltpu.HBM)
    f32, i32 = jnp.float32, jnp.int32
    limit = 60 * 1024 * 1024
    edge = 8 * cx * cy // LANES
    work = pl.pallas_call(
        functools.partial(fill_kernel, (nx, ny, nz)),
        out_shape=(
            jax.ShapeDtypeStruct((4, cx, cy, cz), f32),
            jax.ShapeDtypeStruct((2, 4, 2, cy, cz), f32),
            jax.ShapeDtypeStruct((2, 8 * cx, cz), f32),
            jax.ShapeDtypeStruct((2, edge, LANES), f32),
            jax.ShapeDtypeStruct((cx, cy, cz), f32),
        ),
        in_specs=[hbm] * 9,
        out_specs=(hbm,) * 5,
        scratch_shapes=[
            pltpu.VMEM((4, cx, cy, cz), f32),
            pltpu.VMEM((cx, cy, cz), f32),
            pltpu.VMEM((4, cx, cy, cz), f32),
            pltpu.VMEM((3, 1, points_dev), f32),
            pltpu.SMEM((1,), f32),
            pltpu.VMEM((1, slots), i32),
            pltpu.VMEM((peers, LANES), i32),
            pltpu.VMEM((1, ghosts), i32),
            pltpu.VMEM((8, ghosts), i32),
            pltpu.VMEM((8, ghosts), f32),
            pltpu.VMEM((peers, 4, LANES), f32),
            pltpu.VMEM((peers, 4, LANES), f32),
            pltpu.VMEM((ny, 8, points_dev), f32),
            pltpu.VMEM((cx, cy, LANES), f32),
            pltpu.VMEM((4 * LANES, 2 * ghosts), jnp.bfloat16),
            pltpu.VMEM((2 * cx * cy, peers * LANES), jnp.bfloat16),
            pltpu.VMEM((4 * LANES, 2 * cx * cy), jnp.bfloat16),
            pltpu.VMEM((cx * cy, 2 * ghosts), jnp.bfloat16),
            pltpu.VMEM((LANES, ghosts), jnp.bfloat16),
            pltpu.VMEM((2, 8 * cx, cz), f32),
            pltpu.VMEM((2, edge, LANES), f32),
            pltpu.VMEM((ny * points_dev, cz), f32),
            pltpu.VMEM((ny * points_dev, cz), f32),
            pltpu.VMEM((ny * points_dev, cz), f32),
            pltpu.VMEM((slots, TY, cz), f32),
            pltpu.VMEM((slots, TY, cz), i32),
            pltpu.SemaphoreType.DMA,
            pltpu.SemaphoreType.DMA,
            pltpu.SemaphoreType.DMA((9,)),
            pltpu.SemaphoreType.DMA((peers,)),
            pltpu.SemaphoreType.DMA((peers,)),
            pltpu.SemaphoreType.DMA((ny,)),
            pltpu.SemaphoreType.DMA((ny,)),
            pltpu.SemaphoreType.DMA((6,)),
            pltpu.SemaphoreType.DMA((6,)),
        ],
        compiler_params=pltpu.CompilerParams(
            collective_id=0, has_side_effects=True, vmem_limit_bytes=limit
        ),
    )(
        velocity,
        nu_tilde,
        jnp.transpose(surface, (0, 2, 1, 3))[0],
        pitch_angle,
        near_tiles[0, 0],
        send_rows[0, 0, 0],
        ghost_cell[0, 0],
        ghost_src[0, 0, 0],
        ghost_weight[0, 0, 0],
    )
    return pl.pallas_call(
        functools.partial(step_kernel, (nx, ny, nz)),
        out_shape=(
            jax.ShapeDtypeStruct(velocity.shape, f32),
            jax.ShapeDtypeStruct(nu_tilde.shape, f32),
            jax.ShapeDtypeStruct(nu_tilde.shape, f32),
        ),
        in_specs=[hbm] * 6,
        out_specs=(hbm,) * 3,
        scratch_shapes=[
            pltpu.VMEM((4, cx + 4, cy + 16, cz), f32),
            pltpu.VMEM((2, 8 * cx, cz), f32),
            pltpu.VMEM((2, edge, LANES), f32),
            pltpu.VMEM((cx, cy, cz), f32),
            pltpu.VMEM((cx, cy, cz), i32),
            pltpu.VMEM((4 * cx * cy // LANES, LANES, LANES), f32),
            pltpu.VMEM((4, cx, cy, cz), f32),
            pltpu.VMEM(velocity.shape, f32),
            pltpu.VMEM(nu_tilde.shape, f32),
            pltpu.SemaphoreType.DMA((3,)),
            pltpu.SemaphoreType.DMA((6,)),
            pltpu.SemaphoreType.DMA,
            pltpu.SemaphoreType.DMA((cx,)),
            pltpu.SemaphoreType.DMA((cx,)),
        ],
        compiler_params=pltpu.CompilerParams(vmem_limit_bytes=limit),
    )(*work, fluid_cells)


def solution(mesh):
    in_specs = (
        P(None, "gx", "gy", "gz"),
        P("gx", "gy", "gz"),
        P("gx", "gy", "gz"),
        P("gx", "gz", None, "gy"),
        P(),
        P("gx", "gy", "gz", None),
        P("gx", "gy", "gz", None, None),
        P("gx", "gy", "gz", None),
        P("gx", "gy", "gz", None, None),
        P("gx", "gy", "gz", None, None),
    )
    out_specs = (P(None, "gx", "gy", "gz"), P("gx", "gy", "gz"), P("gx", "gy", "gz"))
    return jax.shard_map(
        on_device, mesh=mesh, in_specs=in_specs, out_specs=out_specs, check_vma=False
    )
```
